256 devices in a mesh: ctx: 8 (over z), head: 32 (over x, y, core).
Axes of the slice: x: 4, y: 4, z: 8, core: 2. Of those that a mesh axis runs over, the one named last changes fastest.
Arguments:
- queries: bfloat16 [16384, 4096], P('ctx', 'head'), may hold values from -6 to 6
- keys: bfloat16 [16384, 1024], P('ctx', 'head'), may hold values from -6 to 6
- values: bfloat16 [16384, 1024], P('ctx', 'head'), may hold values from -6 to 6
- out_weight: bfloat16 [4096, 4096], P('head'), may hold values from -1.5 to 1.5
- doc_starts: int32 [16], replicated, may hold values from 0 to 16383, as said below
Outputs:
- mixed: bfloat16 [16384, 4096], P(('ctx', 'head'))
The draws below stay inside these ranges and needn't reach their ends.
Inputs may be any that keep to these rules, and one draw needn't show every extreme that they name: doc_starts[0] is 0, the entries rise strictly, the last is 16383.
All inputs are finite; a program needn't handle non-finite values.
Results may differ from the reference program's by a relative error of at most 0.024.
Values may be sent and summed in bfloat16 or wider, within the bound.
A program may use at most 128 MiB of HBM per device.

```python
import jax
import jax.numpy as jnp
from jax import lax

D = 4096
HD = 128
GROUP = 4
WINDOW = 4096
TOK_DEV = 2048
H = 32
KVH = 8
TOKENS = 16384
DOCS = 16


def query_key_pair(key):
    parts = jax.random.split(jax.random.fold_in(key, 7), 2)
    query_base = jnp.clip(jax.random.normal(parts[0], (TOKENS, H * HD), jnp.float32), -6.0, 6.0)
    key_base = jnp.clip(jax.random.normal(parts[1], (TOKENS, KVH * HD), jnp.float32), -6.0, 6.0)
    return (query_base, key_base)


def draw_queries(key, part):
    return query_key_pair(key)[0].astype(jnp.bfloat16)


def draw_keys(key, part):
    return query_key_pair(key)[1].astype(jnp.bfloat16)


def draw_doc_starts(key, part):
    shuffled = jax.random.permutation(jax.random.fold_in(key, 3), TOKENS - 2).astype(jnp.int32) + 1
    inner = jnp.sort(shuffled[:DOCS - 2])
    first = jnp.zeros((1,), jnp.int32)
    final = jnp.full((1,), TOKENS - 1, jnp.int32)
    return jnp.concatenate([first, inner, final]).astype(jnp.int32)


def shard_levels(own_key, shape, cuts, smallest, top_value):
    gain, own = 1.0, jax.random.fold_in(own_key, 6)
    for dim, shards_of in cuts:
        draws = jnp.exp(jax.random.uniform(jax.random.fold_in(own, dim), (shards_of,), jnp.float32, smallest / len(cuts), top_value / len(cuts)))
        gain = gain * jnp.repeat(draws, shape[dim] // shards_of).reshape([-1 if axis == dim else 1 for axis in range(len(shape))])
    return gain


def bell_draw(own_key, shape, deviation, limit, cuts=(), kind=jnp.bfloat16):
    gain = shard_levels(own_key, shape, cuts, -0.22, 0.18) if cuts else 1.0
    entries = jax.random.normal(own_key, shape, jnp.float32) * deviation * gain
    return jnp.minimum(jnp.maximum(entries, -limit), limit).astype(kind)


def setup_inputs(seed: int = 0) -> dict:
    key_of = jax.random.split(jax.random.key(seed), 6)
    queries = draw_queries(jax.random.fold_in(key_of[5], 71), 0)
    keys = draw_keys(jax.random.fold_in(key_of[5], 71), 0)
    values = bell_draw(key_of[2], (TOKENS, KVH * HD), 1.0, 6.0, ((0, 8), (1, 32)))
    out_weight = bell_draw(key_of[3], (H * HD, D), (H * HD // 256) ** -0.5, 1.5, ((0, 32),))
    doc_starts = draw_doc_starts(jax.random.fold_in(key_of[5], 71), 0)
    return dict(queries=queries, keys=keys, values=values, out_weight=out_weight, doc_starts=doc_starts)


def doc_index(position, doc_starts):
    return jnp.sum((doc_starts[None, :] <= position[:, None]).astype(jnp.int32), axis=1) - 1


def reference(queries, keys, values, out_weight, doc_starts):
    block_rows = min(512, TOK_DEV)
    scale = HD ** -0.5
    padding = jnp.zeros((WINDOW, KVH * HD), keys.dtype)
    keys_padded = jnp.concatenate([padding, keys], axis=0)
    values_padded = jnp.concatenate([padding, values], axis=0)
    blocks_total = TOKENS // block_rows

    def head_output(head):
        group_col = ((head // GROUP) * HD).astype(jnp.int32)
        query_head = lax.dynamic_slice_in_dim(queries, (head * HD).astype(jnp.int32), HD, 1)
        key_head = lax.dynamic_slice_in_dim(keys_padded, group_col, HD, 1)
        value_head = lax.dynamic_slice_in_dim(values_padded, group_col, HD, 1)

        def one_block(index):
            start = (index * block_rows).astype(jnp.int32)
            query_block = lax.dynamic_slice_in_dim(query_head, start, block_rows, 0)
            key_block = lax.dynamic_slice_in_dim(key_head, start, block_rows + WINDOW, 0)
            value_block = lax.dynamic_slice_in_dim(value_head, start, block_rows + WINDOW, 0)
            query_pos = start + jnp.arange(block_rows, dtype=jnp.int32)
            key_pos = start - WINDOW + jnp.arange(block_rows + WINDOW, dtype=jnp.int32)
            allowed = (key_pos[None, :] >= 0) & (key_pos[None, :] <= query_pos[:, None])
            allowed = allowed & (key_pos[None, :] > query_pos[:, None] - WINDOW)
            allowed = allowed & (doc_index(key_pos, doc_starts)[None, :] == doc_index(query_pos, doc_starts)[:, None])
            scores = lax.dot_general(query_block, key_block, (((1,), (1,)), ((), ())), preferred_element_type=jnp.float32) * scale
            scores = jnp.where(allowed, scores, -1e30)
            row_max = jnp.max(scores, axis=1, keepdims=True)
            weights = jnp.where(allowed, jnp.exp(scores - row_max), 0.0)
            totals = jnp.sum(weights, axis=1, keepdims=True)
            summed = jnp.dot(weights.astype(jnp.bfloat16), value_block, preferred_element_type=jnp.float32)
            return (summed / totals).astype(jnp.bfloat16)

        return lax.map(one_block, jnp.arange(blocks_total, dtype=jnp.int32)).reshape(TOKENS, HD)

    def add_head(total, head):
        attention = head_output(head)
        weight_rows = lax.dynamic_slice_in_dim(out_weight, (head * HD).astype(jnp.int32), HD, 0)
        partial_sum = jnp.dot(attention, weight_rows, preferred_element_type=jnp.float32)
        rounded = lax.optimization_barrier(partial_sum.astype(jnp.bfloat16)).astype(jnp.float32)
        return total + rounded, None

    total, unused = lax.scan(add_head, jnp.zeros((TOKENS, D), jnp.float32), jnp.arange(H, dtype=jnp.int32))
    return total.astype(jnp.bfloat16)
```

```python
import jax
import jax.numpy as jnp
from jax import lax
from jax.experimental import pallas as pl
from jax.experimental.pallas import tpu as pltpu
from jax.sharding import PartitionSpec as P

GROUP = 4
WINDOW = 4096
T = 2048
HD = 128
D = 4096
DOCS = 16
Z, X, Y = 8, 4, 4
HALF = D // 2
NC = 4
CW = HALF // NC
QT = T // X
SUB = QT // Y
TQ = 512
TK = 1024
NEG = -1e30
SCALE = 1.4426950408889634 * HD**-0.5

KV_Z, KV_Y, KV_CA, KV_CB = 0, 3, 6, 9
W_UP, W_DOWN, W_FUP, W_FDOWN, W_SIB = 12, 20, 28, 32, 36
A_X, A_SIB = 37, 40
R_UP, R_DOWN, M_UP, M_DOWN, S_UP, S_DOWN, F_SIB = 44, 48, 52, 56, 60, 64, 68
N_COPIES = 72
L_W, L_ATT, L_OUT = 0, 1, 2
N_LOCAL = 6


def kernel(
    starts_ref, q_ref, k_ref, v_ref, w_ref, out_ref,
    kv, kn, q2, lo_ref, m_ref, acc, obuf, att, wb, part, rel, rin, msg, min_, res,
    ssem, rsem, lsem,
):
    z = lax.axis_index("ctx")
    head = lax.axis_index("head")
    c = lax.rem(head, 2)
    y = lax.rem(head // 2, Y)
    x = head // (2 * Y)
    r = lax.rem(head, GROUP)

    def at(zz, xx, yy, cc):
        return (zz, (xx * Y + yy) * 2 + cc)

    def xx(step):
        return lax.rem(x + step, X)

    def yy(step):
        return lax.rem(y + step, Y)

    z_next = at(lax.rem(z + 1, Z), x, y, c)
    z_prev = at(lax.rem(z + Z - 1, Z), x, y, c)
    sibling = at(z, x, y, 1 - c)
    y_up, y_down = at(z, x, yy(1), c), at(z, x, yy(3), c)
    y_pair = at(z, x, y + 1 - 2 * lax.rem(y, 2), c)

    def copy(src, dst, device, send, recv):
        return pltpu.make_async_remote_copy(
            src_ref=src,
            dst_ref=dst,
            send_sem=ssem.at[send],
            recv_sem=rsem.at[recv],
            device_id=device,
            device_id_type=pl.DeviceIdType.MESH,
        )

    sent = []

    def send(src, dst, device, index, recv=None):
        one = copy(src, dst, device, index, index if recv is None else recv)
        one.start()
        sent.append(one)

    def arrived(dst, index):
        copy(dst, dst, sibling, 0, index).wait_recv()

    def piece(block, member):
        return kv.at[block, :, pl.ds(pl.multiple_of(32 * member, 32), 32), :]

    def w_rows(source_x, source_c):
        return pl.ds(pl.multiple_of(HD * (2 * source_x + source_c), HD), HD)

    def col(start, width):
        return pl.ds(pl.multiple_of(start, 128), width)

    partners = [z_next, z_prev, sibling, y_up, y_down]
    partners += [at(z, xx(1), y, 0), at(z, xx(1), y, 1), at(z, xx(3), y, 0), at(z, xx(3), y, 1)]
    partners += [at(z, xx(2), y, c)]
    barrier = pltpu.get_barrier_semaphore()
    for device in partners:
        pl.semaphore_signal(barrier, inc=1, device_id=device, device_id_type=pl.DeviceIdType.MESH)
    own = pl.ds(pl.multiple_of(32 * r, 32), 32)
    kv[0, 0, own, :] = k_ref[...]
    kv[0, 1, own, :] = v_ref[...]
    pl.semaphore_wait(barrier, len(partners))

    send(piece(0, r), piece(0, r), y_pair, KV_Y)
    send(piece(0, r), piece(1, r), z_next, KV_Z)
    send(piece(0, r), piece(0, r), sibling, KV_CA)
    for k in range(NC):
        for half in range(2):
            src = w_ref.at[:, pl.ds(half * HALF + k * CW, CW)]
            dst = wb.at[w_rows(x, c), pl.ds(k * CW, CW)]
            send(src, dst, at(z, xx(1), y, half), W_UP + 2 * k + half, W_UP + 2 * k + c)
            send(src, dst, at(z, xx(3), y, half), W_DOWN + 2 * k + half, W_DOWN + 2 * k + c)
    send(w_ref.at[:, col((1 - c) * HALF, HALF)], wb.at[w_rows(x, c), :], sibling, W_SIB)
    w_local = pltpu.make_async_copy(
        w_ref.at[:, col(c * HALF, HALF)], wb.at[w_rows(x, c), :], lsem.at[L_W]
    )
    w_local.start()

    def forward_w(k):
        for source_c in range(2):
            arrived(wb.at[w_rows(xx(3), source_c), pl.ds(k * CW, CW)], W_UP + 2 * k + source_c)
        for source_c in range(2):
            arrived(wb.at[w_rows(xx(1), source_c), pl.ds(k * CW, CW)], W_DOWN + 2 * k + source_c)
        below = wb.at[pl.ds(pl.multiple_of(2 * HD * xx(3), 2 * HD), 2 * HD), pl.ds(k * CW, CW // 2)]
        above = wb.at[
            pl.ds(pl.multiple_of(2 * HD * xx(1), 2 * HD), 2 * HD), pl.ds(k * CW + CW // 2, CW // 2)
        ]
        send(below, below, at(z, xx(1), y, c), W_FUP + k)
        send(above, above, at(z, xx(3), y, c), W_FDOWN + k)

    scaled = q_ref[...].astype(jnp.float32).T * SCALE
    coarse = scaled.astype(jnp.bfloat16)
    q2[:HD] = coarse
    q2[HD:] = (scaled - coarse.astype(jnp.float32)).astype(jnp.bfloat16)
    base = z * T
    local = lax.broadcasted_iota(jnp.int32, (8, T), 1)
    begin = jnp.zeros((8, T), jnp.int32)
    for d in range(DOCS):
        start = starts_ref[d]
        begin = jnp.where(local + base >= start, start, begin)
    lo_ref[...] = jnp.maximum(begin - base + WINDOW, local + 1)

    def scores(block, offset, k0, q0, n_sub, width, diagonal):
        keys = kn[block, pl.ds(k0, TK), :]
        keys = jnp.concatenate([keys, keys], axis=1)
        values = jnp.concatenate(
            [kv[block, 1, :, pl.ds(k0, TK)], jnp.ones((16, TK), jnp.bfloat16)], axis=0
        )
        tiles = []
        for u in range(n_sub):
            columns = pl.ds(q0 + u * width, width)
            tiles.append(jnp.dot(keys, q2[:, columns], preferred_element_type=jnp.float32))
        for u in range(n_sub):
            columns = pl.ds(q0 + u * width, width)
            place = lax.broadcasted_iota(jnp.int32, (TK, width), 0)
            allowed = place >= lo_ref[:1, columns] - (offset + k0)
            if diagonal:
                query = lax.broadcasted_iota(jnp.int32, (1, width), 1) + (q0 + u * width - k0)
                allowed &= place <= query
            tile = jnp.where(allowed, tiles[u], NEG)
            top = jnp.max(tile, axis=0, keepdims=True)
            if not diagonal:
                before = m_ref[:1, columns]
                top = jnp.maximum(before, top)
                keep = jnp.exp2(before - top)
            weights = jnp.exp2(tile - top).astype(jnp.bfloat16)
            added = jnp.dot(values, weights, preferred_element_type=jnp.float32)
            m_ref[:1, columns] = top
            acc[:, columns] = added if diagonal else acc[:, columns] * keep + added

    arrived(piece(0, r ^ 2), KV_Y)
    send(piece(0, r ^ 2), piece(0, r ^ 2), sibling, KV_CB)
    arrived(piece(1, r), KV_Z)
    send(piece(1, r), piece(1, r), y_pair, KV_Y + 1)
    send(piece(1, r), piece(2, r), z_next, KV_Z + 1)
    send(piece(1, r), piece(1, r), sibling, KV_CA + 1)
    arrived(piece(0, r ^ 1), KV_CA)
    arrived(piece(0, r ^ 3), KV_CB)
    kn[0] = kv[0, 0].T

    @pl.loop(0, T // TK)
    def _(i):
        q0 = pl.multiple_of(i * TK, TK)
        scores(0, WINDOW, q0, q0, TK // TQ, TQ, True)

        @pl.loop(0, i)
        def _(k):
            scores(0, WINDOW, pl.multiple_of(k * TK, TK), q0, TK // TQ, TQ, False)

    arrived(piece(2, r), KV_Z + 1)
    send(piece(2, r), piece(2, r), y_pair, KV_Y + 2)
    send(piece(2, r), piece(2, r), sibling, KV_CA + 2)
    arrived(piece(1, r ^ 2), KV_Y + 1)
    send(piece(1, r ^ 2), piece(1, r ^ 2), sibling, KV_CB + 1)
    forward_w(0)
    arrived(piece(1, r ^ 1), KV_CA + 1)
    arrived(piece(1, r ^ 3), KV_CB + 1)
    kn[1] = kv[1, 0].T

    for i in range(T // TK):

        @pl.loop(0, T // TK)
        def _(k):
            scores(1, T, pl.multiple_of(k * TK, TK), i * TK, TK // TQ, TQ, False)

        forward_w(1 + i)
        if i == 0:
            arrived(piece(2, r ^ 2), KV_Y + 2)
            send(piece(2, r ^ 2), piece(2, r ^ 2), sibling, KV_CB + 2)

    arrived(piece(2, r ^ 1), KV_CA + 2)
    arrived(piece(2, r ^ 3), KV_CB + 2)
    kn[2] = kv[2, 0].T

    att_own = att.at[:, w_rows(x, c)]
    for i, step in enumerate((2, 1, 3, 0)):
        quarter = xx(step)
        q0 = pl.multiple_of(quarter * QT, QT)

        @pl.loop(q0 // TK, T // TK)
        def _(k):
            scores(2, 0, pl.multiple_of(k * TK, TK), q0, 2, QT // 2, False)

        columns = pl.ds(q0, QT)
        total = acc[HD : HD + 1, columns]
        obuf[i] = (acc[:HD, columns] * (1.0 / total)).T.astype(jnp.bfloat16)
        if step:
            send(obuf.at[i], att_own, at(z, quarter, y, c), A_X + step - 1)
        else:
            send(obuf.at[i], att_own, sibling, A_SIB)
            att_local = pltpu.make_async_copy(obuf.at[i], att_own, lsem.at[L_ATT])
            att_local.start()
    forward_w(3)
    for step in (2, 1, 3):
        slot = att.at[:, w_rows(xx(4 - step), c)]
        arrived(slot, A_X + step - 1)
        send(slot, slot, sibling, A_SIB + step)
    arrived(att.at[:, w_rows(x, 1 - c)], A_SIB)
    for step in (2, 1, 3):
        arrived(att.at[:, w_rows(xx(4 - step), 1 - c)], A_SIB + step)
    att_local.wait()
    w_local.wait()
    arrived(wb.at[w_rows(x, 1 - c), :], W_SIB)

    left, right = pl.ds(0, CW // 2), pl.ds(CW // 2, CW // 2)

    def sub(k, block, half):
        return part[k, pl.ds(pl.multiple_of(block * SUB, SUB), SUB), half]

    def project(k):
        rows = pl.ds(pl.multiple_of(2 * HD * xx(2), 2 * HD), 2 * HD)
        arrived(wb.at[rows, pl.ds(k * CW, CW // 2)], W_FUP + k)
        arrived(wb.at[rows, pl.ds(k * CW + CW // 2, CW // 2)], W_FDOWN + k)
        part[k] = jnp.dot(
            att[...], wb[:, pl.ds(k * CW, CW)], preferred_element_type=jnp.float32
        )
        rel[k, 0] = sub(k, yy(2), left).astype(jnp.bfloat16)
        rel[k, 1] = sub(k, yy(2), right).astype(jnp.bfloat16)
        send(rel.at[k, 0], rin.at[k, 0], y_up, R_UP + k)
        send(rel.at[k, 1], rin.at[k, 1], y_down, R_DOWN + k)
        msg[k, 0] = sub(k, yy(1), right).astype(jnp.bfloat16)
        msg[k, 1] = sub(k, yy(3), left).astype(jnp.bfloat16)
        send(msg.at[k, 0], min_.at[k, 0], y_up, M_UP + k)
        send(msg.at[k, 1], min_.at[k, 1], y_down, M_DOWN + k)

    def relay(k):
        arrived(rin.at[k, 0], R_UP + k)
        msg[k, 2] = (sub(k, yy(1), left) + rin[k, 0].astype(jnp.float32)).astype(jnp.bfloat16)
        send(msg.at[k, 2], min_.at[k, 2], y_up, S_UP + k)
        arrived(rin.at[k, 1], R_DOWN + k)
        msg[k, 3] = (sub(k, yy(3), right) + rin[k, 1].astype(jnp.float32)).astype(jnp.bfloat16)
        send(msg.at[k, 3], min_.at[k, 3], y_down, S_DOWN + k)

    kept = []

    def finish(k):
        arrived(min_.at[k, 0], M_UP + k)
        arrived(min_.at[k, 1], M_DOWN + k)
        arrived(min_.at[k, 2], S_UP + k)
        arrived(min_.at[k, 3], S_DOWN + k)
        for half, columns, near, far in ((0, left, 1, 2), (1, right, 0, 3)):
            total = sub(k, y, columns) + min_[k, near].astype(jnp.float32)
            total += min_[k, far].astype(jnp.float32)
            res[k, :, columns] = total.astype(jnp.bfloat16)
        place = out_ref.at[:, col(c * HALF + k * CW, CW)]
        rows = SUB // 2
        one = pltpu.make_async_copy(
            res.at[k, pl.ds(pl.multiple_of(c * rows, rows), rows), :], place, lsem.at[L_OUT + k]
        )
        one.start()
        kept.append(one)
        send(
            res.at[k, pl.ds(pl.multiple_of((1 - c) * rows, rows), rows), :], place, sibling, F_SIB + k
        )

    for k in range(NC + 2):
        if k < NC:
            project(k)
        if 1 <= k <= NC:
            relay(k - 1)
        if k >= 2:
            finish(k - 2)
    for k in range(NC):
        arrived(out_ref.at[:, col((1 - c) * HALF + k * CW, CW)], F_SIB + k)
    for one in kept:
        one.wait()
    for one in sent:
        one.wait_send()


def on_device(queries, keys, values, out_weight, doc_starts):
    bf16, f32 = jnp.bfloat16, jnp.float32
    vmem = pl.BlockSpec(memory_space=pltpu.VMEM)
    return pl.pallas_call(
        kernel,
        out_shape=jax.ShapeDtypeStruct((SUB // 2, D), bf16),
        in_specs=[pl.BlockSpec(memory_space=pltpu.SMEM), vmem, vmem, vmem, vmem],
        out_specs=pl.BlockSpec(memory_space=pl.ANY),
        scratch_shapes=[
            pltpu.VMEM((3, 2, HD, T), bf16),
            pltpu.VMEM((3, T, HD), bf16),
            pltpu.VMEM((2 * HD, T), bf16),
            pltpu.VMEM((8, T), jnp.int32),
            pltpu.VMEM((8, T), f32),
            pltpu.VMEM((HD + 16, T), f32),
            pltpu.VMEM((X, QT, HD), bf16),
            pltpu.VMEM((QT, 2 * X * HD), bf16),
            pltpu.VMEM((2 * X * HD, HALF), bf16),
            pltpu.VMEM((NC, QT, CW), f32),
            pltpu.VMEM((NC, 2, SUB, CW // 2), bf16),
            pltpu.VMEM((NC, 2, SUB, CW // 2), bf16),
            pltpu.VMEM((NC, 4, SUB, CW // 2), bf16),
            pltpu.VMEM((NC, 4, SUB, CW // 2), bf16),
            pltpu.VMEM((NC, SUB, CW), bf16),
            pltpu.SemaphoreType.DMA((N_COPIES,)),
            pltpu.SemaphoreType.DMA((N_COPIES,)),
            pltpu.SemaphoreType.DMA((N_LOCAL,)),
        ],
        compiler_params=pltpu.CompilerParams(
            collective_id=0, has_side_effects=True, vmem_limit_bytes=56 * 2**20
        ),
    )(doc_starts, queries, keys.T, values.T, out_weight)


def solution(mesh):
    placed = (P("ctx", "head"), P("ctx", "head"), P("ctx", "head"), P("head", None), P())
    return jax.shard_map(
        on_device, mesh=mesh, in_specs=placed, out_specs=P(("ctx", "head"), None), check_vma=False
    )
```

```python
import jax
import jax.numpy as jnp
from jax import lax
from jax.experimental import pallas as pl
from jax.experimental.pallas import tpu as pltpu
from jax.sharding import PartitionSpec as P

GROUP = 4
WINDOW = 4096
T = 2048
HD = 128
D = 4096
DOCS = 16
Z, X, Y = 8, 4, 4
HALF = D // 2
PATH = HALF // 2
CW = 512
NC = PATH // CW
QT = T // X
SUB = QT // Y
TQ = 512
TK = 1024
NEG = -1e30
SCALE = 1.4426950408889634 * HD**-0.5

KV_Y0, KV_Y1, KV_Y2, KV_Z1, KV_Z2A, KV_Z2B = 0, 2, 4, 5, 7, 9
KV_CA, KV_CB, KV_CB2 = 10, 13, 15
W_UP, W_DOWN, W_FUP, W_FDOWN, W_SIB = 17, 21, 25, 27, 29
V_IN, V_OUT, V_FIN, V_FOUT, V_ZUP, V_ZDOWN = 31, 33, 35, 36, 37, 40
A_X, A_Y, A_XSIB, A_YSIB = 43, 46, 58, 62
R_UP = 66
N_COPIES = R_UP + 7 * 2 * NC
L_W, L_ATT, L_OUT = 0, 2, 7
N_LOCAL = L_OUT + 2 * NC


def kernel(
    starts_ref, q_ref, k_ref, v_ref, w_ref, out_ref,
    kv, kn, q2, lo_ref, m_ref, acc, obuf, att, wb, part, rel, rin, msg, min_, res,
    ssem, rsem, lsem,
):
    z = lax.axis_index("ctx")
    head = lax.axis_index("head")
    c = lax.rem(head, 2)
    y = lax.rem(head // 2, Y)
    x = head // (2 * Y)
    r = lax.rem(head, GROUP)
    odd_y, odd_z = lax.rem(y, 2), lax.rem(z, 2)

    def at(z_, x_, y_, c_):
        return (z_, (x_ * Y + y_) * 2 + c_)

    def xx(step):
        return lax.rem(x + step, X)

    def yy(step):
        return lax.rem(y + step, Y)

    z_next = at(lax.rem(z + 1, Z), x, y, c)
    z_prev = at(lax.rem(z + Z - 1, Z), x, y, c)
    sibling = at(z, x, y, 1 - c)
    inner = yy(1 + 2 * odd_y)
    outer = yy(3 - 2 * odd_y)
    y_pair = at(z, x, inner, c)

    def copy(src, dst, device, send, recv):
        return pltpu.make_async_remote_copy(
            src_ref=src,
            dst_ref=dst,
            send_sem=ssem.at[send],
            recv_sem=rsem.at[recv],
            device_id=device,
            device_id_type=pl.DeviceIdType.MESH,
        )

    sent = []
    kept = []

    def send(src, dst, device, index, recv=None):
        one = copy(src, dst, device, index, index if recv is None else recv)
        one.start()
        sent.append(one)

    def keep(src, dst, index):
        one = pltpu.make_async_copy(src, dst, lsem.at[index])
        one.start()
        kept.append(one)

    def arrived(dst, index):
        copy(dst, dst, sibling, 0, index).wait_recv()

    def piece(block, member, which=None):
        rows = pl.ds(pl.multiple_of(32 * member, 32), 32)
        return kv.at[block, :, rows, :] if which is None else kv.at[block, which, rows, :]

    def w_rows(place, core):
        return pl.ds(pl.multiple_of(HD * (2 * place + core), HD), HD)

    def w_pair(place):
        return pl.ds(pl.multiple_of(2 * HD * place, 2 * HD), 2 * HD)

    def col(start, width):
        return pl.ds(pl.multiple_of(start, 128), width)

    partners = [z_next, z_prev, sibling]
    partners += [at(z, x, yy(step), core) for step in (1, 3) for core in range(2)]
    partners += [at(z, xx(step), y, core) for step in (1, 3) for core in range(2)]
    partners += [at(z, x, yy(2), c), at(z, xx(2), y, c)]
    barrier = pltpu.get_barrier_semaphore()
    for device in partners:
        pl.semaphore_signal(barrier, inc=1, device_id=device, device_id_type=pl.DeviceIdType.MESH)
    own = pl.ds(pl.multiple_of(32 * r, 32), 32)
    kv[0, 0, own, :] = k_ref[...]
    kv[0, 1, own, :] = v_ref[...]
    pl.semaphore_wait(barrier, len(partners))

    for which in range(2):
        send(piece(0, r, which), piece(0, r, which), y_pair, KV_Y0 + which)
        send(piece(0, r, which), piece(1, r, which), z_next, KV_Z1 + which)
    send(piece(0, r), piece(0, r), sibling, KV_CA)
    wx, wy = wb.at[0], wb.at[1]
    for k in range(NC):
        for half in range(2):
            src = w_ref.at[:, pl.ds(half * HALF + k * CW, CW)]
            dst = wx.at[w_rows(x, c), pl.ds(k * CW, CW)]
            send(src, dst, at(z, xx(1), y, half), W_UP + 2 * k + half, W_UP + 2 * k + c)
            send(src, dst, at(z, xx(3), y, half), W_DOWN + 2 * k + half, W_DOWN + 2 * k + c)
    mine, theirs = odd_z * (PATH // 2), (1 - odd_z) * (PATH // 2)
    quad = PATH // 4

    def send_wy(place, first):
        for half in range(2):
            src = w_ref.at[:, col(half * HALF + PATH + mine, PATH // 2)]
            dst = wy.at[w_rows(y, c), col(mine, PATH // 2)]
            send(src, dst, at(z, x, place, half), first + half, first + c)

    send_wy(outer, V_OUT)
    for path, place in ((0, x), (1, y)):
        rows = w_rows(place, c)
        send(w_ref.at[:, col((1 - c) * HALF + path * PATH, PATH)], wb.at[path, rows, :], sibling, W_SIB + path)
        keep(w_ref.at[:, col(c * HALF + path * PATH, PATH)], wb.at[path, rows, :], L_W + path)

    def forward_wx(k):
        for core in range(2):
            arrived(wx.at[w_rows(xx(3), core), pl.ds(k * CW, CW)], W_UP + 2 * k + core)
        for core in range(2):
            arrived(wx.at[w_rows(xx(1), core), pl.ds(k * CW, CW)], W_DOWN + 2 * k + core)
        below = wx.at[w_pair(xx(3)), pl.ds(k * CW, CW // 2)]
        above = wx.at[w_pair(xx(1)), pl.ds(k * CW + CW // 2, CW // 2)]
        send(below, below, at(z, xx(1), y, c), W_FUP + k)
        send(above, above, at(z, xx(3), y, c), W_FDOWN + k)

    def share_wy(place, group):
        first = wy.at[w_pair(place), col(mine, quad)]
        second = wy.at[w_pair(place), col(mine + quad, quad)]
        send(second, second, z_next, V_ZUP + group)
        send(first, first, z_prev, V_ZDOWN + group)

    def forward_wy_outer():
        for core in range(2):
            arrived(wy.at[w_rows(outer, core), col(mine, PATH // 2)], V_OUT + core)
        part_b = wy.at[w_pair(outer), col(mine + quad, quad)]
        send(part_b, part_b, y_pair, V_FIN)
        share_wy(outer, 0)

    def forward_wy_inner():
        for core in range(2):
            arrived(wy.at[w_rows(inner, core), col(mine, PATH // 2)], V_IN + core)
        part_a = wy.at[w_pair(inner), col(mine, quad)]
        send(part_a, part_a, at(z, x, outer, c), V_FOUT)
        share_wy(inner, 1)

    def forward_wy_far():
        arrived(wy.at[w_pair(yy(2)), col(mine + quad, quad)], V_FIN)
        arrived(wy.at[w_pair(yy(2)), col(mine, quad)], V_FOUT)
        share_wy(yy(2), 2)

    scaled = q_ref[...].astype(jnp.float32).T * SCALE
    coarse = scaled.astype(jnp.bfloat16)
    q2[:HD] = coarse
    q2[HD:] = (scaled - coarse.astype(jnp.float32)).astype(jnp.bfloat16)
    base = z * T
    local = lax.broadcasted_iota(jnp.int32, (8, T), 1)
    begin = jnp.zeros((8, T), jnp.int32)
    for d in range(DOCS):
        start = starts_ref[d]
        begin = jnp.where(local + base >= start, start, begin)
    lo_ref[...] = jnp.maximum(begin - base + WINDOW, local + 1)

    def scores(block, offset, k0, q0, n_sub, width, diagonal):
        keys = kn[block, pl.ds(k0, TK), :]
        keys = jnp.concatenate([keys, keys], axis=1)
        values = jnp.concatenate(
            [kv[block, 1, :, pl.ds(k0, TK)], jnp.ones((16, TK), jnp.bfloat16)], axis=0
        )
        tiles = []
        for u in range(n_sub):
            columns = pl.ds(q0 + u * width, width)
            tiles.append(jnp.dot(keys, q2[:, columns], preferred_element_type=jnp.float32))
        for u in range(n_sub):
            columns = pl.ds(q0 + u * width, width)
            place = lax.broadcasted_iota(jnp.int32, (TK, width), 0)
            allowed = place >= lo_ref[:1, columns] - (offset + k0)
            if diagonal:
                query = lax.broadcasted_iota(jnp.int32, (1, width), 1) + (q0 + u * width - k0)
                allowed &= place <= query
            tile = jnp.where(allowed, tiles[u], NEG)
            top = jnp.max(tile, axis=0, keepdims=True)
            if not diagonal:
                before = m_ref[:1, columns]
                top = jnp.maximum(before, top)
                keep_ = jnp.exp2(before - top)
            weights = jnp.exp2(tile - top).astype(jnp.bfloat16)
            added = jnp.dot(values, weights, preferred_element_type=jnp.float32)
            m_ref[:1, columns] = top
            acc[:, columns] = added if diagonal else acc[:, columns] * keep_ + added

    arrived(piece(0, r ^ 2, 0), KV_Y0)
    arrived(piece(0, r ^ 2, 1), KV_Y0 + 1)
    send(piece(0, r ^ 2), piece(0, r ^ 2), sibling, KV_CB)
    arrived(piece(1, r, 0), KV_Z1)
    arrived(piece(1, r, 1), KV_Z1 + 1)
    for which in range(2):
        send(piece(1, r, which), piece(1, r, which), y_pair, KV_Y1 + which)
        send(piece(1, r, 1 - which), piece(2, r, 1 - which), z_next, KV_Z2A + 1 - which)
    send(piece(1, r), piece(1, r), sibling, KV_CA + 1)
    arrived(piece(0, r ^ 1), KV_CA)
    arrived(piece(0, r ^ 3), KV_CB)
    kn[0] = kv[0, 0].T

    @pl.loop(0, T // TK)
    def _(i):
        q0 = pl.multiple_of(i * TK, TK)
        scores(0, WINDOW, q0, q0, TK // TQ, TQ, True)

        @pl.loop(0, i)
        def _(k):
            scores(0, WINDOW, pl.multiple_of(k * TK, TK), q0, TK // TQ, TQ, False)

    arrived(piece(1, r ^ 2, 0), KV_Y1)
    send(piece(1, r ^ 2, 0), piece(2, r ^ 2, 0), z_next, KV_Z2B)
    arrived(piece(2, r, 1), KV_Z2A + 1)
    send(piece(2, r, 1), piece(2, r, 1), y_pair, KV_Y2)
    arrived(piece(1, r ^ 2, 1), KV_Y1 + 1)
    send(piece(1, r ^ 2), piece(1, r ^ 2), sibling, KV_CB + 1)
    arrived(piece(2, r, 0), KV_Z2A)
    send(piece(2, r), piece(2, r), sibling, KV_CA + 2)
    send_wy(inner, V_IN)
    forward_wx(0)
    arrived(piece(1, r ^ 1), KV_CA + 1)
    arrived(piece(1, r ^ 3), KV_CB + 1)
    kn[1] = kv[1, 0].T

    for i in range(T // TK):

        @pl.loop(0, T // TK)
        def _(k):
            scores(1, T, pl.multiple_of(k * TK, TK), i * TK, TK // TQ, TQ, False)

        if i == 0:
            arrived(piece(2, r ^ 2, 0), KV_Z2B)
            send(piece(2, r ^ 2, 0), piece(2, r ^ 2, 0), sibling, KV_CB2)
            arrived(piece(2, r ^ 2, 1), KV_Y2)
            send(piece(2, r ^ 2, 1), piece(2, r ^ 2, 1), sibling, KV_CB2 + 1)
            forward_wx(1)
            forward_wy_outer()

    arrived(piece(2, r ^ 1), KV_CA + 2)
    arrived(piece(2, r ^ 3, 0), KV_CB2)
    arrived(piece(2, r ^ 3, 1), KV_CB2 + 1)
    kn[2] = kv[2, 0].T

    att_x, att_y = att.at[0], att.at[1]
    x_slot, y_slot = w_rows(x, c), w_rows(y, c)

    def sub_rows(place):
        return pl.ds(pl.multiple_of(place * SUB, SUB), SUB)

    for i, step in enumerate((2, 1, 3, 0)):
        quarter = xx(step)
        q0 = pl.multiple_of(quarter * QT, QT)

        @pl.loop(q0 // TK, T // TK)
        def _(k):
            scores(2, 0, pl.multiple_of(k * TK, TK), q0, 2, QT // 2, False)

        columns = pl.ds(q0, QT)
        total = acc[HD : HD + 1, columns]
        obuf[i] = (acc[:HD, columns] * (1.0 / total)).T.astype(jnp.bfloat16)
        if step:
            send(obuf.at[i], att_x.at[:, x_slot], at(z, quarter, y, c), A_X + step - 1)
        else:
            send(obuf.at[i], att_x.at[:, x_slot], sibling, A_XSIB)
            keep(obuf.at[i], att_x.at[:, x_slot], L_ATT)
        for away in (2, 1, 3):
            send(
                obuf.at[i, sub_rows(yy(away)), :],
                att_y.at[sub_rows(quarter), y_slot],
                at(z, x, yy(away), c),
                A_Y + 4 * (away - 1) + step,
            )
        keep(obuf.at[i, sub_rows(y), :], att_y.at[sub_rows(quarter), y_slot], L_ATT + 1 + i)
        if i == 1:
            forward_wy_inner()
    for one in kept[-5:]:
        one.wait()
    send(att_y.at[:, y_slot], att_y.at[:, y_slot], sibling, A_YSIB)
    for step in (2, 1, 3):
        slot = att_x.at[:, w_rows(xx(4 - step), c)]
        arrived(slot, A_X + step - 1)
        send(slot, slot, sibling, A_XSIB + step)
        slot = w_rows(yy(4 - step), c)
        for quarter in range(X):
            arrived(att_y.at[sub_rows(xx(quarter)), slot], A_Y + 4 * (step - 1) + quarter)
        send(att_y.at[:, slot], att_y.at[:, slot], sibling, A_YSIB + step)
    forward_wy_far()
    arrived(wx.at[w_rows(x, 1 - c), :], W_SIB)
    arrived(wy.at[w_rows(y, 1 - c), :], W_SIB + 1)
    for one in kept[:2]:
        one.wait()
    for step in range(4):
        arrived(att_x.at[:, w_rows(xx(4 - step), 1 - c)], A_XSIB + step)
    for step in range(4):
        arrived(att_y.at[:, w_rows(yy(4 - step), 1 - c)], A_YSIB + step)

    left, right = pl.ds(0, CW // 2), pl.ds(CW // 2, CW // 2)
    away = (yy, xx)

    def device(path, step):
        return at(z, x, yy(step), c) if path == 0 else at(z, xx(step), y, c)

    def chunk_of(path, k):
        return k * CW if path == 0 else (mine if k == 0 else theirs)

    def sub(j, block, half):
        return part[j, sub_rows(block), half]

    def project(path, k):
        j = 2 * k + path
        if path == 0:
            arrived(wx.at[w_pair(xx(2)), pl.ds(k * CW, CW // 2)], W_FUP + k)
            arrived(wx.at[w_pair(xx(2)), pl.ds(k * CW + CW // 2, CW // 2)], W_FDOWN + k)
        elif k == 1:
            for group, place in enumerate((outer, inner, yy(2))):
                arrived(wy.at[w_pair(place), col(theirs + quad, quad)], V_ZUP + group)
                arrived(wy.at[w_pair(place), col(theirs, quad)], V_ZDOWN + group)
        near, step = away[path], R_UP + 7 * j
        weight = wb[path, :, col(chunk_of(path, k), CW)]
        part[j] = jnp.dot(att[path], weight, preferred_element_type=jnp.float32)
        rel[j, 0] = sub(j, near(2), left).astype(jnp.bfloat16)
        send(rel.at[j, 0], rin.at[j, 0], device(path, 1), step)
        rel[j, 1] = sub(j, near(2), right).astype(jnp.bfloat16)
        send(rel.at[j, 1], rin.at[j, 1], device(path, 3), step + 1)
        msg[j, 0] = sub(j, near(1), right).astype(jnp.bfloat16)
        send(msg.at[j, 0], min_.at[j, 0], device(path, 1), step + 2)
        msg[j, 1] = sub(j, near(3), left).astype(jnp.bfloat16)
        send(msg.at[j, 1], min_.at[j, 1], device(path, 3), step + 3)

    def relay(path, k):
        j = 2 * k + path
        near, step = away[path], R_UP + 7 * j
        arrived(rin.at[j, 0], step)
        msg[j, 2] = (sub(j, near(1), left) + rin[j, 0].astype(jnp.float32)).astype(jnp.bfloat16)
        send(msg.at[j, 2], min_.at[j, 2], device(path, 1), step + 4)
        arrived(rin.at[j, 1], step + 1)
        msg[j, 3] = (sub(j, near(3), right) + rin[j, 1].astype(jnp.float32)).astype(jnp.bfloat16)
        send(msg.at[j, 3], min_.at[j, 3], device(path, 3), step + 5)

    def finish(path, k):
        j = 2 * k + path
        step = R_UP + 7 * j
        for one in range(4):
            arrived(min_.at[j, one], step + 2 + one)
        for columns, first, second in ((left, 1, 2), (right, 0, 3)):
            total = sub(j, x if path else y, columns) + min_[j, first].astype(jnp.float32)
            total += min_[j, second].astype(jnp.float32)
            res[j, :, columns] = total.astype(jnp.bfloat16)
        place = out_ref.at[:, col(c * HALF + path * PATH + chunk_of(path, k), CW)]
        rows = SUB // 2
        keep(res.at[j, pl.ds(pl.multiple_of(c * rows, rows), rows), :], place, L_OUT + j)
        other = pl.ds(pl.multiple_of((1 - c) * rows, rows), rows)
        send(res.at[j, other, :], place, sibling, step + 6)

    order = [(path, k) for k in range(NC) for path in range(2)]
    for n in range(len(order) + 4):
        if n < len(order):
            project(*order[n])
        if 2 <= n < len(order) + 2:
            relay(*order[n - 2])
        if n >= 4:
            finish(*order[n - 4])
    for path, k in order:
        place = out_ref.at[:, col((1 - c) * HALF + path * PATH + chunk_of(path, k), CW)]
        arrived(place, R_UP + 7 * (2 * k + path) + 6)
    for one in kept[-len(order) :]:
        one.wait()
    for one in sent:
        one.wait_send()


def on_device(queries, keys, values, out_weight, doc_starts):
    bf16, f32 = jnp.bfloat16, jnp.float32
    vmem = pl.BlockSpec(memory_space=pltpu.VMEM)
    return pl.pallas_call(
        kernel,
        out_shape=jax.ShapeDtypeStruct((SUB // 2, D), bf16),
        in_specs=[pl.BlockSpec(memory_space=pltpu.SMEM), vmem, vmem, vmem, vmem],
        out_specs=pl.BlockSpec(memory_space=pl.ANY),
        scratch_shapes=[
            pltpu.VMEM((3, 2, HD, T), bf16),
            pltpu.VMEM((3, T, HD), bf16),
            pltpu.VMEM((2 * HD, T), bf16),
            pltpu.VMEM((8, T), jnp.int32),
            pltpu.VMEM((8, T), f32),
            pltpu.VMEM((HD + 16, T), f32),
            pltpu.VMEM((X, QT, HD), bf16),
            pltpu.VMEM((2, QT, 2 * X * HD), bf16),
            pltpu.VMEM((2, 2 * X * HD, PATH), bf16),
            pltpu.VMEM((2 * NC, QT, CW), f32),
            pltpu.VMEM((2 * NC, 2, SUB, CW // 2), bf16),
            pltpu.VMEM((2 * NC, 2, SUB, CW // 2), bf16),
            pltpu.VMEM((2 * NC, 4, SUB, CW // 2), bf16),
            pltpu.VMEM((2 * NC, 4, SUB, CW // 2), bf16),
            pltpu.VMEM((2 * NC, SUB, CW), bf16),
            pltpu.SemaphoreType.DMA((N_COPIES,)),
            pltpu.SemaphoreType.DMA((N_COPIES,)),
            pltpu.SemaphoreType.DMA((N_LOCAL,)),
        ],
        compiler_params=pltpu.CompilerParams(
            collective_id=0, has_side_effects=True, vmem_limit_bytes=56 * 2**20
        ),
    )(doc_starts, queries, keys.T, values.T, out_weight)


def solution(mesh):
    placed = (P("ctx", "head"), P("ctx", "head"), P("ctx", "head"), P("head", None), P())
    return jax.shard_map(
        on_device, mesh=mesh, in_specs=placed, out_specs=P(("ctx", "head"), None), check_vma=False
    )
```

```python
import jax
import jax.numpy as jnp
from jax import lax
from jax.experimental import pallas as pl
from jax.experimental.pallas import tpu as pltpu
from jax.sharding import PartitionSpec as P

GROUP = 4
WINDOW = 4096
T = 2048
HD = 128
D = 4096
DOCS = 16
Z, X, Y = 8, 4, 4
HALF = D // 2
PATH = HALF // 2
CW = 512
NC = PATH // CW
QT = T // X
SUB = QT // Y
TQ = 512
TK = 1024
NEG = -1e30
SCALE = 1.4426950408889634 * HD**-0.5

ORDER = (2, 1, 3, 0)

KV_Y0, KV_Y1, KV_Y2, KV_Z1, KV_Z2A, KV_Z2B = 0, 2, 4, 5, 7, 9
KV_CA0, KV_CB0, KV_CA1, KV_CB1, KV_CA2, KV_CB2 = 10, 12, 14, 15, 16, 17
W_UP, W_DOWN, W_FUP, W_FDOWN, W_SIB = 19, 23, 27, 29, 31
V_IN, V_OUT, V_FIN, V_FOUT, V_ZUP, V_ZDOWN, V_ZEDGE = 33, 35, 37, 38, 39, 42, 45
A_X, A_Y, A_XSIB, A_YOWN, A_YF = 48, 51, 63, 67, 71
R_UP = 77
N_COPIES = R_UP + 7 * 2 * NC
L_W, L_ATT, L_OUT = 0, 2, 7
N_LOCAL = L_OUT + 2 * NC


def kernel(
    starts_ref, q_ref, k_ref, v_ref, w_ref, out_ref,
    kv, kn, q2, lo_ref, m_ref, acc, obuf, att, wb, part, rel, rin, msg, min_, res,
    ssem, rsem, lsem,
):
    z = lax.axis_index("ctx")
    head = lax.axis_index("head")
    c = lax.rem(head, 2)
    y = lax.rem(head // 2, Y)
    x = head // (2 * Y)
    r = lax.rem(head, GROUP)
    odd_y, odd_z = lax.rem(y, 2), lax.rem(z, 2)

    def at(z_, x_, y_, c_):
        return (z_, (x_ * Y + y_) * 2 + c_)

    def xx(step):
        return lax.rem(x + step, X)

    def yy(step):
        return lax.rem(y + step, Y)

    z_next = at(lax.rem(z + 1, Z), x, y, c)
    z_prev = at(lax.rem(z + Z - 1, Z), x, y, c)
    has_next, has_one, has_two = z < Z - 1, z >= 1, z >= 2
    sibling = at(z, x, y, 1 - c)
    inner = yy(1 + 2 * odd_y)
    outer = yy(3 - 2 * odd_y)
    y_pair = at(z, x, inner, c)

    def copy(src, dst, device, send, recv):
        return pltpu.make_async_remote_copy(
            src_ref=src,
            dst_ref=dst,
            send_sem=ssem.at[send],
            recv_sem=rsem.at[recv],
            device_id=device,
            device_id_type=pl.DeviceIdType.MESH,
        )

    def do(action, when):
        if when is None:
            action()
        else:
            pl.when(when)(action)

    sent = []
    kept = []

    def send(src, dst, device, index, recv=None, when=None):
        one = copy(src, dst, device, index, index if recv is None else recv)
        do(one.start, when)
        sent.append((one, when))

    def keep(src, dst, index):
        one = pltpu.make_async_copy(src, dst, lsem.at[index])
        one.start()
        kept.append(one)

    def arrived(dst, index, when=None):
        do(copy(dst, dst, sibling, 0, index).wait_recv, when)

    def piece(block, member, which=None, half=None):
        rows = pl.ds(pl.multiple_of(32 * member, 32), 32)
        tokens = pl.ds(0, T) if half is None else pl.ds(half * (T // 2), T // 2)
        return kv.at[block, :, rows, tokens] if which is None else kv.at[block, which, rows, tokens]

    def w_rows(place, core):
        return pl.ds(pl.multiple_of(HD * (2 * place + core), HD), HD)

    def w_pair(place):
        return pl.ds(pl.multiple_of(2 * HD * place, 2 * HD), 2 * HD)

    def col(start, width):
        return pl.ds(pl.multiple_of(start, 128), width)

    partners = [(sibling, None), (z_next, has_next), (z_prev, has_one)]
    partners += [(at(z, x, yy(step), core), None) for step in (1, 3) for core in range(2)]
    partners += [(at(z, xx(step), y, core), None) for step in (1, 3) for core in range(2)]
    partners += [(at(z, x, yy(2), c), None), (at(z, xx(2), y, c), None)]
    barrier = pltpu.get_barrier_semaphore()
    for device, when in partners:

        def greet(device=device):
            pl.semaphore_signal(barrier, inc=1, device_id=device, device_id_type=pl.DeviceIdType.MESH)

        do(greet, when)
    own = pl.ds(pl.multiple_of(32 * r, 32), 32)
    kv[0, 0, own, :] = k_ref[...]
    kv[0, 1, own, :] = v_ref[...]
    at_edge = jnp.where(has_next, 0, 1) + jnp.where(has_one, 0, 1)
    pl.semaphore_wait(barrier, len(partners) - at_edge)

    send(piece(0, r, half=0), piece(0, r, half=0), y_pair, KV_Y0)
    send(piece(0, r, 0), piece(1, r, 0), z_next, KV_Z1, when=has_next)
    send(piece(0, r, half=0), piece(0, r, half=0), sibling, KV_CA0)
    send(piece(0, r, half=1), piece(0, r, half=1), y_pair, KV_Y0 + 1)
    send(piece(0, r, 1), piece(1, r, 1), z_next, KV_Z1 + 1, when=has_next)
    send(piece(0, r, half=1), piece(0, r, half=1), sibling, KV_CA0 + 1)
    wx, wy = wb.at[0], wb.at[1]
    for k in range(NC):
        for half in range(2):
            src = w_ref.at[:, pl.ds(half * HALF + k * CW, CW)]
            dst = wx.at[w_rows(x, c), pl.ds(k * CW, CW)]
            send(src, dst, at(z, xx(1), y, half), W_UP + 2 * k + half, W_UP + 2 * k + c)
            send(src, dst, at(z, xx(3), y, half), W_DOWN + 2 * k + half, W_DOWN + 2 * k + c)
    mine, theirs = odd_z * (PATH // 2), (1 - odd_z) * (PATH // 2)
    quad = PATH // 4

    def send_wy(place, first):
        for half in range(2):
            src = w_ref.at[:, col(half * HALF + PATH + mine, PATH // 2)]
            dst = wy.at[w_rows(y, c), col(mine, PATH // 2)]
            send(src, dst, at(z, x, place, half), first + half, first + c)

    send_wy(outer, V_OUT)
    for path, place in ((0, x), (1, y)):
        rows = w_rows(place, c)
        send(w_ref.at[:, col((1 - c) * HALF + path * PATH, PATH)], wb.at[path, rows, :], sibling, W_SIB + path)
        keep(w_ref.at[:, col(c * HALF + path * PATH, PATH)], wb.at[path, rows, :], L_W + path)

    def forward_wx(k):
        for core in range(2):
            arrived(wx.at[w_rows(xx(3), core), pl.ds(k * CW, CW)], W_UP + 2 * k + core)
        for core in range(2):
            arrived(wx.at[w_rows(xx(1), core), pl.ds(k * CW, CW)], W_DOWN + 2 * k + core)
        below = wx.at[w_pair(xx(3)), pl.ds(k * CW, CW // 2)]
        above = wx.at[w_pair(xx(1)), pl.ds(k * CW + CW // 2, CW // 2)]
        send(below, below, at(z, xx(1), y, c), W_FUP + k)
        send(above, above, at(z, xx(3), y, c), W_FDOWN + k)

    def share_wy(place, group):
        first = wy.at[w_pair(place), col(mine, quad)]
        second = wy.at[w_pair(place), col(mine + quad, quad)]
        send(second, second, z_next, V_ZUP + group, when=has_next)
        send(first, first, z_prev, V_ZDOWN + group, when=has_one)
        send(second, second, z_prev, V_ZEDGE + group, V_ZUP + group, when=z == 1)
        up = copy(first, first, z_next, V_ZEDGE + group, V_ZDOWN + group)
        do(up.start, z == Z - 2)
        sent.append((up, z == Z - 2))

    def forward_wy_outer():
        for core in range(2):
            arrived(wy.at[w_rows(outer, core), col(mine, PATH // 2)], V_OUT + core)
        part_b = wy.at[w_pair(outer), col(mine + quad, quad)]
        send(part_b, part_b, y_pair, V_FIN)
        share_wy(outer, 0)

    def forward_wy_inner():
        for core in range(2):
            arrived(wy.at[w_rows(inner, core), col(mine, PATH // 2)], V_IN + core)
        part_a = wy.at[w_pair(inner), col(mine, quad)]
        send(part_a, part_a, at(z, x, outer, c), V_FOUT)
        share_wy(inner, 1)

    def forward_wy_far():
        arrived(wy.at[w_pair(yy(2)), col(mine + quad, quad)], V_FIN)
        arrived(wy.at[w_pair(yy(2)), col(mine, quad)], V_FOUT)
        share_wy(yy(2), 2)

    scaled = q_ref[...].astype(jnp.float32).T * SCALE
    coarse = scaled.astype(jnp.bfloat16)
    q2[:HD] = coarse
    q2[HD:] = (scaled - coarse.astype(jnp.float32)).astype(jnp.bfloat16)
    base = z * T
    local = lax.broadcasted_iota(jnp.int32, (8, T), 1)
    begin = jnp.zeros((8, T), jnp.int32)
    for d in range(DOCS):
        start = starts_ref[d]
        begin = jnp.where(local + base >= start, start, begin)
    lo_ref[...] = jnp.maximum(begin - base + WINDOW, local + 1)

    def scores(block, offset, k0, q0, width, span=TK, diagonal=False):
        keys = kn[block, pl.ds(k0, span), :]
        keys = jnp.concatenate([keys, keys], axis=1)
        values = jnp.concatenate(
            [kv[block, 1, :, pl.ds(k0, span)], jnp.ones((16, span), jnp.bfloat16)], axis=0
        )
        tiles = []
        spans = [(u + 1) * width if diagonal else span for u in range(2)]
        for u in range(2):
            columns = pl.ds(q0 + u * width, width)
            tiles.append(
                jnp.dot(keys[: spans[u]], q2[:, columns], preferred_element_type=jnp.float32)
            )
        for u in range(2):
            columns = pl.ds(q0 + u * width, width)
            place = lax.broadcasted_iota(jnp.int32, (spans[u], width), 0)
            allowed = place >= lo_ref[:1, columns] - (offset + k0)
            if diagonal:
                query = lax.broadcasted_iota(jnp.int32, (1, width), 1) + (q0 + u * width - k0)
                allowed &= place <= query
            tile = jnp.where(allowed, tiles[u], NEG)
            top = jnp.max(tile, axis=0, keepdims=True)
            if not diagonal:
                before = m_ref[:1, columns]
                top = jnp.maximum(before, top)
                keep_ = jnp.exp2(before - top)
            weights = jnp.exp2(tile - top).astype(jnp.bfloat16)
            added = jnp.dot(values[:, : spans[u]], weights, preferred_element_type=jnp.float32)
            m_ref[:1, columns] = top
            acc[:, columns] = added if diagonal else acc[:, columns] * keep_ + added

    half_t = T // 2
    arrived(piece(0, r ^ 2, half=0), KV_Y0)
    send(piece(0, r ^ 2, half=0), piece(0, r ^ 2, half=0), sibling, KV_CB0)
    arrived(piece(1, r, 0), KV_Z1, when=has_one)
    send(piece(1, r, 0), piece(1, r, 0), y_pair, KV_Y1, when=has_one)
    send(piece(1, r, 0), piece(2, r, 0), z_next, KV_Z2A, when=has_one & has_next)
    arrived(piece(0, r ^ 1, half=0), KV_CA0)
    arrived(piece(0, r ^ 3, half=0), KV_CB0)
    kn[0, pl.ds(0, half_t)] = kv[0, 0, :, pl.ds(0, half_t)].T
    scores(0, WINDOW, 0, 0, TQ, diagonal=True)
    arrived(piece(0, r ^ 2, half=1), KV_Y0 + 1)
    send(piece(0, r ^ 2, half=1), piece(0, r ^ 2, half=1), sibling, KV_CB0 + 1)
    arrived(piece(1, r, 1), KV_Z1 + 1, when=has_one)
    send(piece(1, r, 1), piece(1, r, 1), y_pair, KV_Y1 + 1, when=has_one)
    send(piece(1, r, 1), piece(2, r, 1), z_next, KV_Z2A + 1, when=has_one & has_next)
    send(piece(1, r), piece(1, r), sibling, KV_CA1, when=has_one)
    arrived(piece(0, r ^ 1, half=1), KV_CA0 + 1)
    arrived(piece(0, r ^ 3, half=1), KV_CB0 + 1)
    kn[0, pl.ds(half_t, half_t)] = kv[0, 0, :, pl.ds(half_t, half_t)].T
    scores(0, WINDOW, half_t, half_t, TQ, diagonal=True)
    arrived(piece(1, r ^ 2, 0), KV_Y1, when=has_one)
    send(piece(1, r ^ 2, 0), piece(2, r ^ 2, 0), z_next, KV_Z2B, when=has_one & has_next)
    scores(0, WINDOW, 0, half_t, TQ)

    arrived(piece(2, r, 1), KV_Z2A + 1, when=has_two)
    send(piece(2, r, 1), piece(2, r, 1), y_pair, KV_Y2, when=has_two)
    arrived(piece(1, r ^ 2, 1), KV_Y1 + 1, when=has_one)
    send(piece(1, r ^ 2), piece(1, r ^ 2), sibling, KV_CB1, when=has_one)
    arrived(piece(2, r, 0), KV_Z2A, when=has_two)
    send(piece(2, r), piece(2, r), sibling, KV_CA2, when=has_two)
    send_wy(inner, V_IN)
    forward_wx(0)
    arrived(piece(1, r ^ 1), KV_CA1, when=has_one)
    arrived(piece(1, r ^ 3), KV_CB1, when=has_one)

    for i in range(T // TK):

        @pl.when(has_one)
        def _():
            if i == 0:
                kn[1] = kv[1, 0].T

            @pl.loop(0, T // TK)
            def _(k):
                scores(1, T, pl.multiple_of(k * TK, TK), i * TK, TQ)

        if i == 0:
            for which, index in ((0, KV_Z2B), (1, KV_Y2)):
                arrived(piece(2, r ^ 2, which), index, when=has_two)
                send(piece(2, r ^ 2, which), piece(2, r ^ 2, which), sibling, KV_CB2 + which, when=has_two)
            forward_wx(1)
            forward_wy_outer()

    arrived(piece(2, r ^ 1), KV_CA2, when=has_two)
    arrived(piece(2, r ^ 3, 0), KV_CB2, when=has_two)
    arrived(piece(2, r ^ 3, 1), KV_CB2 + 1, when=has_two)

    @pl.when(has_two)
    def _():
        kn[2] = kv[2, 0].T

    att_x, att_y = att.at[0], att.at[1]
    x_slot, y_slot = w_rows(x, c), w_rows(y, c)

    def sub_rows(place):
        return pl.ds(pl.multiple_of(place * SUB, SUB), SUB)

    def forward_x(step):
        slot = att_x.at[:, w_rows(xx(4 - step), c)]
        arrived(slot, A_X + step - 1)
        send(slot, slot, sibling, A_XSIB + step)

    def forward_y(step, half):
        slot = w_rows(yy(4 - step), c)
        for i in (2 * half, 2 * half + 1):
            arrived(att_y.at[sub_rows(i), slot], A_Y + 4 * (step - 1) + i)
        both = att_y.at[pl.ds(2 * SUB * half, 2 * SUB), slot]
        send(both, both, sibling, A_YF + 2 * (step - 1) + half)

    for i, step in enumerate(ORDER):
        quarter = xx(step)
        q0 = pl.multiple_of(quarter * QT, QT)

        @pl.when(has_two & (lax.rem(quarter, 2) == 1))
        def _():
            scores(2, 0, q0, q0, QT // 2, span=QT)

        @pl.when(has_two)
        def _():
            @pl.loop((quarter + 1) // 2, T // TK)
            def _(k):
                scores(2, 0, pl.multiple_of(k * TK, TK), q0, QT // 2)

        columns = pl.ds(q0, QT)
        total = acc[HD : HD + 1, columns]
        obuf[i] = (acc[:HD, columns] * (1.0 / total)).T.astype(jnp.bfloat16)
        if step:
            send(obuf.at[i], att_x.at[:, x_slot], at(z, quarter, y, c), A_X + step - 1)
        else:
            send(obuf.at[i], att_x.at[:, x_slot], sibling, A_XSIB)
            keep(obuf.at[i], att_x.at[:, x_slot], L_ATT)
        for away in (2, 1, 3):
            send(
                obuf.at[i, sub_rows(yy(away)), :],
                att_y.at[sub_rows(i), y_slot],
                at(z, x, yy(away), c),
                A_Y + 4 * (away - 1) + i,
            )
        send(obuf.at[i, sub_rows(y), :], att_y.at[sub_rows(i), y_slot], sibling, A_YOWN + i)
        keep(obuf.at[i, sub_rows(y), :], att_y.at[sub_rows(i), y_slot], L_ATT + 1 + i)
        if i == 1:
            forward_wy_inner()
        if i == 2:
            forward_x(2)
            for away in (2, 1, 3):
                forward_y(away, 0)
    for away in (1, 3):
        forward_x(away)
    for away in (2, 1, 3):
        forward_y(away, 1)
    forward_wy_far()
    arrived(wx.at[w_rows(x, 1 - c), :], W_SIB)
    arrived(wy.at[w_rows(y, 1 - c), :], W_SIB + 1)
    for one in kept:
        one.wait()
    del kept[:]
    for step in range(4):
        arrived(att_x.at[:, w_rows(xx(4 - step), 1 - c)], A_XSIB + step)

    left, right = pl.ds(0, CW // 2), pl.ds(CW // 2, CW // 2)
    def device(path, step):
        return at(z, x, yy(step), c) if path == 0 else at(z, xx(step), y, c)

    def chunk_of(path, k):
        return k * CW if path == 0 else (mine if k == 0 else theirs)

    def sub(j, block, half):
        return part[j, sub_rows(block), half]

    def block_of(path, step):
        return yy(step) if path == 0 else ORDER.index(step)

    def project(path, k):
        j = 2 * k + path
        if path == 0:
            arrived(wx.at[w_pair(xx(2)), pl.ds(k * CW, CW // 2)], W_FUP + k)
            arrived(wx.at[w_pair(xx(2)), pl.ds(k * CW + CW // 2, CW // 2)], W_FDOWN + k)
        elif k == 1:
            for group, place in enumerate((outer, inner, yy(2))):
                arrived(wy.at[w_pair(place), col(theirs + quad, quad)], V_ZUP + group)
                arrived(wy.at[w_pair(place), col(theirs, quad)], V_ZDOWN + group)
        step = R_UP + 7 * j
        if path == 1 and k == 0:
            for i in range(4):
                arrived(att_y.at[sub_rows(i), w_rows(y, 1 - c)], A_YOWN + i)
            for away in (1, 2, 3):
                for half in range(2):
                    both = att_y.at[pl.ds(2 * SUB * half, 2 * SUB), w_rows(yy(4 - away), 1 - c)]
                    arrived(both, A_YF + 2 * (away - 1) + half)
        weight = wb[path, :, col(chunk_of(path, k), CW)]
        part[j] = jnp.dot(att[path], weight, preferred_element_type=jnp.float32)
        rel[j, 0] = sub(j, block_of(path, 2), left).astype(jnp.bfloat16)
        send(rel.at[j, 0], rin.at[j, 0], device(path, 1), step)
        rel[j, 1] = sub(j, block_of(path, 2), right).astype(jnp.bfloat16)
        send(rel.at[j, 1], rin.at[j, 1], device(path, 3), step + 1)
        msg[j, 0] = sub(j, block_of(path, 1), right).astype(jnp.bfloat16)
        send(msg.at[j, 0], min_.at[j, 0], device(path, 1), step + 2)
        msg[j, 1] = sub(j, block_of(path, 3), left).astype(jnp.bfloat16)
        send(msg.at[j, 1], min_.at[j, 1], device(path, 3), step + 3)

    def relay(path, k):
        j = 2 * k + path
        step = R_UP + 7 * j
        arrived(rin.at[j, 0], step)
        msg[j, 2] = (sub(j, block_of(path, 1), left) + rin[j, 0].astype(jnp.float32)).astype(jnp.bfloat16)
        send(msg.at[j, 2], min_.at[j, 2], device(path, 1), step + 4)
        arrived(rin.at[j, 1], step + 1)
        msg[j, 3] = (sub(j, block_of(path, 3), right) + rin[j, 1].astype(jnp.float32)).astype(jnp.bfloat16)
        send(msg.at[j, 3], min_.at[j, 3], device(path, 3), step + 5)

    def finish(path, k):
        j = 2 * k + path
        step = R_UP + 7 * j
        for one in range(4):
            arrived(min_.at[j, one], step + 2 + one)
        for columns, first, second in ((left, 1, 2), (right, 0, 3)):
            total = sub(j, block_of(path, 0), columns) + min_[j, first].astype(jnp.float32)
            total += min_[j, second].astype(jnp.float32)
            res[j, :, columns] = total.astype(jnp.bfloat16)
        place = out_ref.at[:, col(c * HALF + path * PATH + chunk_of(path, k), CW)]
        rows = SUB // 2
        keep(res.at[j, pl.ds(pl.multiple_of(c * rows, rows), rows), :], place, L_OUT + j)
        other = pl.ds(pl.multiple_of((1 - c) * rows, rows), rows)
        send(res.at[j, other, :], place, sibling, step + 6)

    order = [(path, k) for k in range(NC) for path in range(2)]
    for n in range(len(order) + 4):
        if n < len(order):
            project(*order[n])
        if 2 <= n < len(order) + 2:
            relay(*order[n - 2])
        if n >= 4:
            finish(*order[n - 4])
    for path, k in order:
        place = out_ref.at[:, col((1 - c) * HALF + path * PATH + chunk_of(path, k), CW)]
        arrived(place, R_UP + 7 * (2 * k + path) + 6)
    for one in kept:
        one.wait()
    for one, when in sent:
        do(one.wait_send, when)


def on_device(queries, keys, values, out_weight, doc_starts):
    bf16, f32 = jnp.bfloat16, jnp.float32
    vmem = pl.BlockSpec(memory_space=pltpu.VMEM)
    return pl.pallas_call(
        kernel,
        out_shape=jax.ShapeDtypeStruct((SUB // 2, D), bf16),
        in_specs=[pl.BlockSpec(memory_space=pltpu.SMEM), vmem, vmem, vmem, vmem],
        out_specs=pl.BlockSpec(memory_space=pl.ANY),
        scratch_shapes=[
            pltpu.VMEM((3, 2, HD, T), bf16),
            pltpu.VMEM((3, T, HD), bf16),
            pltpu.VMEM((2 * HD, T), bf16),
            pltpu.VMEM((8, T), jnp.int32),
            pltpu.VMEM((8, T), f32),
            pltpu.VMEM((HD + 16, T), f32),
            pltpu.VMEM((X, QT, HD), bf16),
            pltpu.VMEM((2, QT, 2 * X * HD), bf16),
            pltpu.VMEM((2, 2 * X * HD, PATH), bf16),
            pltpu.VMEM((2 * NC, QT, CW), f32),
            pltpu.VMEM((2 * NC, 2, SUB, CW // 2), bf16),
            pltpu.VMEM((2 * NC, 2, SUB, CW // 2), bf16),
            pltpu.VMEM((2 * NC, 4, SUB, CW // 2), bf16),
            pltpu.VMEM((2 * NC, 4, SUB, CW // 2), bf16),
            pltpu.VMEM((2 * NC, SUB, CW), bf16),
            pltpu.SemaphoreType.DMA((N_COPIES,)),
            pltpu.SemaphoreType.DMA((N_COPIES,)),
            pltpu.SemaphoreType.DMA((N_LOCAL,)),
        ],
        compiler_params=pltpu.CompilerParams(
            collective_id=0, has_side_effects=True, vmem_limit_bytes=56 * 2**20
        ),
    )(doc_starts, queries, keys.T, values.T, out_weight)


def solution(mesh):
    placed = (P("ctx", "head"), P("ctx", "head"), P("ctx", "head"), P("head", None), P())
    return jax.shard_map(
        on_device, mesh=mesh, in_specs=placed, out_specs=P(("ctx", "head"), None), check_vma=False
    )
```

```python
import jax
import jax.numpy as jnp
from jax import lax
from jax.experimental import pallas as pl
from jax.experimental.pallas import tpu as pltpu
from jax.sharding import PartitionSpec as P

GROUP = 4
WINDOW = 4096
T = 2048
HD = 128
D = 4096
DOCS = 16
Z, X, Y = 8, 4, 4
HALF = D // 2
PATH = HALF // 2
CW = 256
NC = PATH // CW
WC = 512
QT = T // X
SUB = QT // Y
TQ = 512
TK = 1024
NEG = -1e30
SCALE = 1.4426950408889634 * HD**-0.5

ORDER = (2, 1, 3, 0)

KV_Y0, KV_Y1, KV_Z1, KV_Z2, KV_FAR = 0, 2, 4, 6, 8
KV_CA, KV_CB = 10, 16
W_UP, W_DOWN, W_FUP, W_FDOWN, W_SIB = 22, 26, 30, 32, 34
V_IN, V_OUT, V_FIN, V_FOUT, V_ZUP, V_ZDOWN, V_ZEDGE = 36, 38, 40, 41, 42, 45, 48
A_X, A_Y, A_XSIB, A_YOWN, A_YF = 51, 54, 66, 70, 74
R_UP = 80
N_COPIES = R_UP + 7 * 2 * NC
L_W, L_ATT, L_OUT = 0, 2, 7
N_LOCAL = L_OUT + 2 * NC


def kernel(
    starts_ref, q_ref, k_ref, v_ref, w_ref, out_ref,
    kv, kn, q2, lo_ref, m_ref, acc, obuf, att, wb, part, rel, rin, msg, min_, res,
    ssem, rsem, lsem,
):
    z = lax.axis_index("ctx")
    head = lax.axis_index("head")
    c = lax.rem(head, 2)
    y = lax.rem(head // 2, Y)
    x = head // (2 * Y)
    r = lax.rem(head, GROUP)
    odd_y, odd_z = lax.rem(y, 2), lax.rem(z, 2)

    def at(z_, x_, y_, c_):
        return (z_, (x_ * Y + y_) * 2 + c_)

    def xx(step):
        return lax.rem(x + step, X)

    def yy(step):
        return lax.rem(y + step, Y)

    z_next = at(lax.rem(z + 1, Z), x, y, c)
    z_prev = at(lax.rem(z + Z - 1, Z), x, y, c)
    has_next, has_one, has_two = z < Z - 1, z >= 1, z >= 2
    sibling = at(z, x, y, 1 - c)
    inner = yy(1 + 2 * odd_y)
    outer = yy(3 - 2 * odd_y)
    y_pair = at(z, x, inner, c)

    def copy(src, dst, device, send, recv):
        return pltpu.make_async_remote_copy(
            src_ref=src,
            dst_ref=dst,
            send_sem=ssem.at[send],
            recv_sem=rsem.at[recv],
            device_id=device,
            device_id_type=pl.DeviceIdType.MESH,
        )

    def do(action, when):
        if when is None:
            action()
        else:
            pl.when(when)(action)

    sent = []
    kept = []

    def send(src, dst, device, index, recv=None, when=None):
        one = copy(src, dst, device, index, index if recv is None else recv)
        do(one.start, when)
        sent.append((one, when))

    def keep(src, dst, index):
        one = pltpu.make_async_copy(src, dst, lsem.at[index])
        one.start()
        kept.append(one)

    def arrived(dst, index, when=None):
        do(copy(dst, dst, sibling, 0, index).wait_recv, when)

    def piece(block, member, half):
        rows = pl.ds(pl.multiple_of(32 * member, 32), 32)
        tokens = pl.ds(half * (T // 2), T // 2)
        return kv.at[block, :, rows, tokens]

    def w_rows(place, core):
        return pl.ds(pl.multiple_of(HD * (2 * place + core), HD), HD)

    def w_pair(place):
        return pl.ds(pl.multiple_of(2 * HD * place, 2 * HD), 2 * HD)

    def col(start, width):
        return pl.ds(pl.multiple_of(start, 128), width)

    partners = [(sibling, None), (z_next, has_next), (z_prev, has_one)]
    partners += [(at(z, x, yy(step), core), None) for step in (1, 3) for core in range(2)]
    partners += [(at(z, xx(step), y, core), None) for step in (1, 3) for core in range(2)]
    partners += [(at(z, x, yy(2), c), None), (at(z, xx(2), y, c), None)]
    barrier = pltpu.get_barrier_semaphore()
    for device, when in partners:

        def greet(device=device):
            pl.semaphore_signal(barrier, inc=1, device_id=device, device_id_type=pl.DeviceIdType.MESH)

        do(greet, when)
    own = pl.ds(pl.multiple_of(32 * r, 32), 32)
    kv[0, 0, own, :] = k_ref[...]
    kv[0, 1, own, :] = v_ref[...]
    at_edge = jnp.where(has_next, 0, 1) + jnp.where(has_one, 0, 1)
    pl.semaphore_wait(barrier, len(partners) - at_edge)

    for h in range(2):
        send(piece(0, r, h), piece(0, r, h), y_pair, KV_Y0 + h)
        send(piece(0, r, h), piece(1, r, h), z_next, KV_Z1 + h, when=has_next)
        send(piece(0, r, h), piece(0, r, h), sibling, KV_CA + h)
    wx, wy = wb.at[0], wb.at[1]
    for k in range(2):
        for half in range(2):
            src = w_ref.at[:, pl.ds(half * HALF + k * WC, WC)]
            dst = wx.at[w_rows(x, c), pl.ds(k * WC, WC)]
            send(src, dst, at(z, xx(1), y, half), W_UP + 2 * k + half, W_UP + 2 * k + c)
            send(src, dst, at(z, xx(3), y, half), W_DOWN + 2 * k + half, W_DOWN + 2 * k + c)
    mine, theirs = odd_z * (PATH // 2), (1 - odd_z) * (PATH // 2)
    quad = PATH // 4

    def send_wy(place, first):
        for half in range(2):
            src = w_ref.at[:, col(half * HALF + PATH + mine, PATH // 2)]
            dst = wy.at[w_rows(y, c), col(mine, PATH // 2)]
            send(src, dst, at(z, x, place, half), first + half, first + c)

    send_wy(outer, V_OUT)
    for path, place in ((0, x), (1, y)):
        rows = w_rows(place, c)
        send(w_ref.at[:, col((1 - c) * HALF + path * PATH, PATH)], wb.at[path, rows, :], sibling, W_SIB + path)
        keep(w_ref.at[:, col(c * HALF + path * PATH, PATH)], wb.at[path, rows, :], L_W + path)

    def forward_wx(k):
        for core in range(2):
            arrived(wx.at[w_rows(xx(3), core), pl.ds(k * WC, WC)], W_UP + 2 * k + core)
        for core in range(2):
            arrived(wx.at[w_rows(xx(1), core), pl.ds(k * WC, WC)], W_DOWN + 2 * k + core)
        below = wx.at[w_pair(xx(3)), pl.ds(k * WC, WC // 2)]
        above = wx.at[w_pair(xx(1)), pl.ds(k * WC + WC // 2, WC // 2)]
        send(below, below, at(z, xx(1), y, c), W_FUP + k)
        send(above, above, at(z, xx(3), y, c), W_FDOWN + k)

    def share_wy(place, group):
        first = wy.at[w_pair(place), col(mine, quad)]
        second = wy.at[w_pair(place), col(mine + quad, quad)]
        send(second, second, z_next, V_ZUP + group, when=has_next)
        send(first, first, z_prev, V_ZDOWN + group, when=has_one)
        send(second, second, z_prev, V_ZEDGE + group, V_ZUP + group, when=z == 1)
        send(first, first, z_next, V_ZEDGE + group, V_ZDOWN + group, when=z == Z - 2)

    def forward_wy_outer():
        for core in range(2):
            arrived(wy.at[w_rows(outer, core), col(mine, PATH // 2)], V_OUT + core)
        part_b = wy.at[w_pair(outer), col(mine + quad, quad)]
        send(part_b, part_b, y_pair, V_FIN)
        share_wy(outer, 0)

    def forward_wy_inner():
        for core in range(2):
            arrived(wy.at[w_rows(inner, core), col(mine, PATH // 2)], V_IN + core)
        part_a = wy.at[w_pair(inner), col(mine, quad)]
        send(part_a, part_a, at(z, x, outer, c), V_FOUT)
        share_wy(inner, 1)

    def forward_wy_far():
        arrived(wy.at[w_pair(yy(2)), col(mine + quad, quad)], V_FIN)
        arrived(wy.at[w_pair(yy(2)), col(mine, quad)], V_FOUT)
        share_wy(yy(2), 2)

    scaled = q_ref[...].astype(jnp.float32).T * SCALE
    coarse = scaled.astype(jnp.bfloat16)
    q2[:HD] = coarse
    q2[HD:] = (scaled - coarse.astype(jnp.float32)).astype(jnp.bfloat16)
    base = z * T
    local = lax.broadcasted_iota(jnp.int32, (8, T), 1)
    begin = jnp.zeros((8, T), jnp.int32)
    for d in range(DOCS):
        start = starts_ref[d]
        begin = jnp.where(local + base >= start, start, begin)
    lo_ref[...] = jnp.maximum(begin - base + WINDOW, local + 1)

    def scores(block, offset, k0, q0, width, span=TK, diagonal=False):
        keys = kn[block, pl.ds(k0, span), :]
        keys = jnp.concatenate([keys, keys], axis=1)
        values = jnp.concatenate(
            [kv[block, 1, :, pl.ds(k0, span)], jnp.ones((16, span), jnp.bfloat16)], axis=0
        )
        tiles = []
        spans = [(u + 1) * width if diagonal else span for u in range(2)]
        for u in range(2):
            columns = pl.ds(q0 + u * width, width)
            tiles.append(
                jnp.dot(keys[: spans[u]], q2[:, columns], preferred_element_type=jnp.float32)
            )
        for u in range(2):
            columns = pl.ds(q0 + u * width, width)
            place = lax.broadcasted_iota(jnp.int32, (spans[u], width), 0)
            allowed = place >= lo_ref[:1, columns] - (offset + k0)
            if diagonal:
                query = lax.broadcasted_iota(jnp.int32, (1, width), 1) + (q0 + u * width - k0)
                allowed &= place <= query
            tile = jnp.where(allowed, tiles[u], NEG)
            top = jnp.max(tile, axis=0, keepdims=True)
            if not diagonal:
                before = m_ref[:1, columns]
                top = jnp.maximum(before, top)
                keep_ = jnp.exp2(before - top)
            weights = jnp.exp2(tile - top).astype(jnp.bfloat16)
            added = jnp.dot(values[:, : spans[u]], weights, preferred_element_type=jnp.float32)
            m_ref[:1, columns] = top
            acc[:, columns] = added if diagonal else acc[:, columns] * keep_ + added

    def turn(block, h):
        half = pl.ds(h * (T // 2), T // 2)
        kn[block, half] = kv[block, 0, :, half].T

    def own_to_sibling(block, h, when):
        send(piece(block, r, h), piece(block, r, h), sibling, KV_CA + 2 * block + h, when=when)

    def pair_to_sibling(block, h, when=None):
        member = r ^ 2
        send(piece(block, member, h), piece(block, member, h), sibling, KV_CB + 2 * block + h, when=when)

    def whole(block, h, when=None):
        arrived(piece(block, r ^ 1, h), KV_CA + 2 * block + h, when=when)
        arrived(piece(block, r ^ 3, h), KV_CB + 2 * block + h, when=when)

    half_t = T // 2
    for h in range(2):
        arrived(piece(0, r ^ 2, h), KV_Y0 + h)
        pair_to_sibling(0, h)
        arrived(piece(1, r, h), KV_Z1 + h, when=has_one)
        send(piece(1, r, h), piece(1, r, h), y_pair, KV_Y1 + h, when=has_one)
        send(piece(1, r, h), piece(2, r, h), z_next, KV_Z2 + h, when=has_one & has_next)
        own_to_sibling(1, h, has_one)
        whole(0, h)
        turn(0, h)
        scores(0, WINDOW, h * half_t, h * half_t, TQ, diagonal=True)
    arrived(piece(1, r ^ 2, 0), KV_Y1, when=has_one)
    send(piece(1, r ^ 2, 0), piece(2, r ^ 2, 0), z_next, KV_FAR, when=has_one & has_next)
    pair_to_sibling(1, 0, has_one)
    arrived(piece(2, r, 0), KV_Z2, when=has_two)
    own_to_sibling(2, 0, has_two)
    scores(0, WINDOW, 0, half_t, TQ)

    whole(1, 0, has_one)

    def before(h, group):
        scores(1, T, h * half_t, group * half_t, TQ)

    @pl.when(has_one)
    def _():
        turn(1, 0)
        before(0, 0)

    arrived(piece(1, r ^ 2, 1), KV_Y1 + 1, when=has_one)
    pair_to_sibling(1, 1, has_one)
    arrived(piece(2, r, 1), KV_Z2 + 1, when=has_two)
    send(piece(2, r, 1), piece(2, r, 1), y_pair, KV_FAR + 1, when=has_two)
    own_to_sibling(2, 1, has_two)
    send_wy(inner, V_IN)

    @pl.when(has_one)
    def _():
        before(0, 1)

    forward_wx(0)
    whole(1, 1, has_one)

    @pl.when(has_one)
    def _():
        turn(1, 1)
        before(1, 0)

    for h in range(2):
        arrived(piece(2, r ^ 2, h), KV_FAR + h, when=has_two)
        pair_to_sibling(2, h, has_two)
    forward_wx(1)
    forward_wy_outer()

    @pl.when(has_one)
    def _():
        before(1, 1)

    for h in range(2):
        whole(2, h, has_two)

    @pl.when(has_two)
    def _():
        turn(2, 0)
        turn(2, 1)

    att_x, att_y = att.at[0], att.at[1]
    x_slot, y_slot = w_rows(x, c), w_rows(y, c)

    def sub_rows(place):
        return pl.ds(pl.multiple_of(place * SUB, SUB), SUB)

    def forward_x(step):
        slot = att_x.at[:, w_rows(xx(4 - step), c)]
        arrived(slot, A_X + step - 1)
        send(slot, slot, sibling, A_XSIB + step)

    def forward_y(step, half):
        slot = w_rows(yy(4 - step), c)
        for i in (2 * half, 2 * half + 1):
            arrived(att_y.at[sub_rows(i), slot], A_Y + 4 * (step - 1) + i)
        both = att_y.at[pl.ds(2 * SUB * half, 2 * SUB), slot]
        send(both, both, sibling, A_YF + 2 * (step - 1) + half)

    for i, step in enumerate(ORDER):
        quarter = xx(step)
        q0 = pl.multiple_of(quarter * QT, QT)

        @pl.when(has_two & (lax.rem(quarter, 2) == 1))
        def _():
            scores(2, 0, q0, q0, QT // 2, span=QT)

        @pl.when(has_two)
        def _():
            @pl.loop((quarter + 1) // 2, T // TK)
            def _(k):
                scores(2, 0, pl.multiple_of(k * TK, TK), q0, QT // 2)

        columns = pl.ds(q0, QT)
        total = acc[HD : HD + 1, columns]
        obuf[i] = (acc[:HD, columns] * (1.0 / total)).T.astype(jnp.bfloat16)
        if step:
            send(obuf.at[i], att_x.at[:, x_slot], at(z, quarter, y, c), A_X + step - 1)
        else:
            send(obuf.at[i], att_x.at[:, x_slot], sibling, A_XSIB)
            keep(obuf.at[i], att_x.at[:, x_slot], L_ATT)
        for away in (2, 1, 3):
            send(
                obuf.at[i, sub_rows(yy(away)), :],
                att_y.at[sub_rows(i), y_slot],
                at(z, x, yy(away), c),
                A_Y + 4 * (away - 1) + i,
            )
        send(obuf.at[i, sub_rows(y), :], att_y.at[sub_rows(i), y_slot], sibling, A_YOWN + i)
        keep(obuf.at[i, sub_rows(y), :], att_y.at[sub_rows(i), y_slot], L_ATT + 1 + i)
        if i == 0:
            forward_wy_inner()
        if i == 2:
            forward_wy_far()
            forward_x(2)
            for away in (2, 1, 3):
                forward_y(away, 0)
    for away in (1, 3):
        forward_x(away)
    for away in (2, 1, 3):
        forward_y(away, 1)
    arrived(wx.at[w_rows(x, 1 - c), :], W_SIB)
    arrived(wy.at[w_rows(y, 1 - c), :], W_SIB + 1)
    for one in kept:
        one.wait()
    del kept[:]
    for step in range(4):
        arrived(att_x.at[:, w_rows(xx(4 - step), 1 - c)], A_XSIB + step)

    left, right = pl.ds(0, CW // 2), pl.ds(CW // 2, CW // 2)
    def device(path, step):
        return at(z, x, yy(step), c) if path == 0 else at(z, xx(step), y, c)

    def chunk_of(path, k):
        if path == 0:
            return k * CW
        return (mine if k < NC // 2 else theirs) + k % (NC // 2) * CW

    def sub(j, block, half):
        return part[j, sub_rows(block), half]

    def block_of(path, step):
        return yy(step) if path == 0 else ORDER.index(step)

    def project(path, k):
        j = 2 * k + path
        if path == 0 and k * CW % WC == 0:
            part_x = k * CW // WC
            arrived(wx.at[w_pair(xx(2)), pl.ds(k * CW, WC // 2)], W_FUP + part_x)
            arrived(wx.at[w_pair(xx(2)), pl.ds(k * CW + WC // 2, WC // 2)], W_FDOWN + part_x)
        elif path == 1 and k == NC // 2:
            for group, place in enumerate((outer, inner, yy(2))):
                arrived(wy.at[w_pair(place), col(theirs + quad, quad)], V_ZUP + group)
                arrived(wy.at[w_pair(place), col(theirs, quad)], V_ZDOWN + group)
        step = R_UP + 7 * j
        if path == 1 and k == 0:
            for i in range(4):
                arrived(att_y.at[sub_rows(i), w_rows(y, 1 - c)], A_YOWN + i)
            for away in (1, 2, 3):
                for half in range(2):
                    both = att_y.at[pl.ds(2 * SUB * half, 2 * SUB), w_rows(yy(4 - away), 1 - c)]
                    arrived(both, A_YF + 2 * (away - 1) + half)
        weight = wb[path, :, col(chunk_of(path, k), CW)]
        part[j] = jnp.dot(att[path], weight, preferred_element_type=jnp.float32)
        rel[j, 0] = sub(j, block_of(path, 2), left).astype(jnp.bfloat16)
        send(rel.at[j, 0], rin.at[j, 0], device(path, 1), step)
        rel[j, 1] = sub(j, block_of(path, 2), right).astype(jnp.bfloat16)
        send(rel.at[j, 1], rin.at[j, 1], device(path, 3), step + 1)

    def relay(path, k):
        j = 2 * k + path
        step = R_UP + 7 * j
        msg[j, 0] = sub(j, block_of(path, 1), right).astype(jnp.bfloat16)
        send(msg.at[j, 0], min_.at[j, 0], device(path, 1), step + 2)
        msg[j, 1] = sub(j, block_of(path, 3), left).astype(jnp.bfloat16)
        send(msg.at[j, 1], min_.at[j, 1], device(path, 3), step + 3)
        arrived(rin.at[j, 0], step)
        msg[j, 2] = (sub(j, block_of(path, 1), left) + rin[j, 0].astype(jnp.float32)).astype(jnp.bfloat16)
        send(msg.at[j, 2], min_.at[j, 2], device(path, 1), step + 4)
        arrived(rin.at[j, 1], step + 1)
        msg[j, 3] = (sub(j, block_of(path, 3), right) + rin[j, 1].astype(jnp.float32)).astype(jnp.bfloat16)
        send(msg.at[j, 3], min_.at[j, 3], device(path, 3), step + 5)

    def finish(path, k):
        j = 2 * k + path
        step = R_UP + 7 * j
        for one in range(4):
            arrived(min_.at[j, one], step + 2 + one)
        for columns, first, second in ((left, 1, 2), (right, 0, 3)):
            total = sub(j, block_of(path, 0), columns) + min_[j, first].astype(jnp.float32)
            total += min_[j, second].astype(jnp.float32)
            res[j, :, columns] = total.astype(jnp.bfloat16)
        place = out_ref.at[:, col(c * HALF + path * PATH + chunk_of(path, k), CW)]
        rows = SUB // 2
        keep(res.at[j, pl.ds(pl.multiple_of(c * rows, rows), rows), :], place, L_OUT + j)
        other = pl.ds(pl.multiple_of((1 - c) * rows, rows), rows)
        send(res.at[j, other, :], place, sibling, step + 6)

    order = [(path, k) for k in range(NC) for path in range(2)]
    lag, last = 3, len(order)
    for n in range(2 * last):
        if n < last:
            project(*order[n])
        if lag <= n < last + lag:
            relay(*order[n - lag])
        if n >= last:
            finish(*order[n - last])
    for path, k in order:
        place = out_ref.at[:, col((1 - c) * HALF + path * PATH + chunk_of(path, k), CW)]
        arrived(place, R_UP + 7 * (2 * k + path) + 6)
    for one in kept:
        one.wait()
    for one, when in sent:
        do(one.wait_send, when)


def on_device(queries, keys, values, out_weight, doc_starts):
    bf16, f32 = jnp.bfloat16, jnp.float32
    vmem = pl.BlockSpec(memory_space=pltpu.VMEM)
    return pl.pallas_call(
        kernel,
        out_shape=jax.ShapeDtypeStruct((SUB // 2, D), bf16),
        in_specs=[pl.BlockSpec(memory_space=pltpu.SMEM), vmem, vmem, vmem, vmem],
        out_specs=pl.BlockSpec(memory_space=pl.ANY),
        scratch_shapes=[
            pltpu.VMEM((3, 2, HD, T), bf16),
            pltpu.VMEM((3, T, HD), bf16),
            pltpu.VMEM((2 * HD, T), bf16),
            pltpu.VMEM((8, T), jnp.int32),
            pltpu.VMEM((8, T), f32),
            pltpu.VMEM((HD + 16, T), f32),
            pltpu.VMEM((X, QT, HD), bf16),
            pltpu.VMEM((2, QT, 2 * X * HD), bf16),
            pltpu.VMEM((2, 2 * X * HD, PATH), bf16),
            pltpu.VMEM((2 * NC, QT, CW), f32),
            pltpu.VMEM((2 * NC, 2, SUB, CW // 2), bf16),
            pltpu.VMEM((2 * NC, 2, SUB, CW // 2), bf16),
            pltpu.VMEM((2 * NC, 4, SUB, CW // 2), bf16),
            pltpu.VMEM((2 * NC, 4, SUB, CW // 2), bf16),
            pltpu.VMEM((2 * NC, SUB, CW), bf16),
            pltpu.SemaphoreType.DMA((N_COPIES,)),
            pltpu.SemaphoreType.DMA((N_COPIES,)),
            pltpu.SemaphoreType.DMA((N_LOCAL,)),
        ],
        compiler_params=pltpu.CompilerParams(
            collective_id=0, has_side_effects=True, vmem_limit_bytes=56 * 2**20
        ),
    )(doc_starts, queries, keys.T, values.T, out_weight)


def solution(mesh):
    placed = (P("ctx", "head"), P("ctx", "head"), P("ctx", "head"), P("head", None), P())
    return jax.shard_map(
        on_device, mesh=mesh, in_specs=placed, out_specs=P(("ctx", "head"), None), check_vma=False
    )
```

```python
import jax
import jax.numpy as jnp
from jax import lax
from jax.experimental import pallas as pl
from jax.experimental.pallas import tpu as pltpu
from jax.sharding import PartitionSpec as P

GROUP = 4
WINDOW = 4096
T = 2048
HD = 128
D = 4096
DOCS = 16
Z, X, Y = 8, 4, 4
HALF = D // 2
PATH = HALF // 2
CW = 512
NC = PATH // CW
QT = T // X
SUB = QT // Y
TQ = 512
TK = 1024
NEG = -1e30
SCALE = 1.4426950408889634 * HD**-0.5

ORDER = (2, 1, 3, 0)

KV_Y0, KV_Y1, KV_Y2, KV_Z1, KV_Z2A, KV_Z2B = 0, 2, 4, 5, 7, 9
KV_CA0, KV_CB0, KV_CA1, KV_CB1, KV_CA2, KV_CB2 = 10, 12, 14, 15, 16, 17
W_UP, W_DOWN, W_FUP, W_FDOWN, W_SIB = 19, 23, 27, 29, 31
V_IN, V_OUT, V_FIN, V_FOUT, V_ZUP, V_ZDOWN, V_ZEDGE = 33, 35, 37, 38, 39, 42, 45
A_X, A_Y, A_XSIB, A_YOWN, A_YF = 48, 51, 63, 67, 71
R_UP = 77
N_COPIES = R_UP + 7 * 2 * NC
L_W, L_ATT, L_OUT = 0, 2, 7
N_LOCAL = L_OUT + 2 * NC


def kernel(
    starts_ref, q_ref, k_ref, v_ref, w_ref, out_ref,
    kv, kn, q2, lo_ref, m_ref, acc, obuf, att, wb, part, rel, rin, msg, min_, res,
    ssem, rsem, lsem,
):
    z = lax.axis_index("ctx")
    head = lax.axis_index("head")
    c = lax.rem(head, 2)
    y = lax.rem(head // 2, Y)
    x = head // (2 * Y)
    r = lax.rem(head, GROUP)
    odd_y, odd_z = lax.rem(y, 2), lax.rem(z, 2)

    def at(z_, x_, y_, c_):
        return (z_, (x_ * Y + y_) * 2 + c_)

    def xx(step):
        return lax.rem(x + step, X)

    def yy(step):
        return lax.rem(y + step, Y)

    z_next = at(lax.rem(z + 1, Z), x, y, c)
    z_prev = at(lax.rem(z + Z - 1, Z), x, y, c)
    has_next, has_one, has_two = z < Z - 1, z >= 1, z >= 2
    sibling = at(z, x, y, 1 - c)
    inner = yy(1 + 2 * odd_y)
    outer = yy(3 - 2 * odd_y)
    y_pair = at(z, x, inner, c)

    def copy(src, dst, device, send, recv):
        return pltpu.make_async_remote_copy(
            src_ref=src,
            dst_ref=dst,
            send_sem=ssem.at[send],
            recv_sem=rsem.at[recv],
            device_id=device,
            device_id_type=pl.DeviceIdType.MESH,
        )

    def do(action, when):
        if when is None:
            action()
        else:
            pl.when(when)(action)

    sent = []
    kept = []

    def send(src, dst, device, index, recv=None, when=None):
        one = copy(src, dst, device, index, index if recv is None else recv)
        do(one.start, when)
        sent.append((one, when))

    def keep(src, dst, index):
        one = pltpu.make_async_copy(src, dst, lsem.at[index])
        one.start()
        kept.append(one)

    def arrived(dst, index, when=None):
        do(copy(dst, dst, sibling, 0, index).wait_recv, when)

    def piece(block, member, which=None, half=None):
        rows = pl.ds(pl.multiple_of(32 * member, 32), 32)
        tokens = pl.ds(0, T) if half is None else pl.ds(half * (T // 2), T // 2)
        return kv.at[block, :, rows, tokens] if which is None else kv.at[block, which, rows, tokens]

    def w_rows(place, core):
        return pl.ds(pl.multiple_of(HD * (2 * place + core), HD), HD)

    def w_pair(place):
        return pl.ds(pl.multiple_of(2 * HD * place, 2 * HD), 2 * HD)

    def col(start, width):
        return pl.ds(pl.multiple_of(start, 128), width)

    partners = [(sibling, None), (z_next, has_next), (z_prev, has_one)]
    partners += [(at(z, x, yy(step), core), None) for step in (1, 3) for core in range(2)]
    partners += [(at(z, xx(step), y, core), None) for step in (1, 3) for core in range(2)]
    partners += [(at(z, x, yy(2), c), None), (at(z, xx(2), y, c), None)]
    barrier = pltpu.get_barrier_semaphore()
    for device, when in partners:

        def greet(device=device):
            pl.semaphore_signal(barrier, inc=1, device_id=device, device_id_type=pl.DeviceIdType.MESH)

        do(greet, when)
    own = pl.ds(pl.multiple_of(32 * r, 32), 32)
    kv[0, 0, own, :] = k_ref[...]
    kv[0, 1, own, :] = v_ref[...]
    at_edge = jnp.where(has_next, 0, 1) + jnp.where(has_one, 0, 1)
    pl.semaphore_wait(barrier, len(partners) - at_edge)

    send(piece(0, r, half=0), piece(0, r, half=0), y_pair, KV_Y0)
    send(piece(0, r, 0), piece(1, r, 0), z_next, KV_Z1, when=has_next)
    send(piece(0, r, half=0), piece(0, r, half=0), sibling, KV_CA0)
    send(piece(0, r, half=1), piece(0, r, half=1), y_pair, KV_Y0 + 1)
    send(piece(0, r, 1), piece(1, r, 1), z_next, KV_Z1 + 1, when=has_next)
    send(piece(0, r, half=1), piece(0, r, half=1), sibling, KV_CA0 + 1)
    wx, wy = wb.at[0], wb.at[1]
    for k in range(NC):
        for half in range(2):
            src = w_ref.at[:, pl.ds(half * HALF + k * CW, CW)]
            dst = wx.at[w_rows(x, c), pl.ds(k * CW, CW)]
            send(src, dst, at(z, xx(1), y, half), W_UP + 2 * k + half, W_UP + 2 * k + c)
            send(src, dst, at(z, xx(3), y, half), W_DOWN + 2 * k + half, W_DOWN + 2 * k + c)
    mine, theirs = odd_z * (PATH // 2), (1 - odd_z) * (PATH // 2)
    quad = PATH // 4

    def send_wy(place, first):
        for half in range(2):
            src = w_ref.at[:, col(half * HALF + PATH + mine, PATH // 2)]
            dst = wy.at[w_rows(y, c), col(mine, PATH // 2)]
            send(src, dst, at(z, x, place, half), first + half, first + c)

    send_wy(outer, V_OUT)
    for path, place in ((0, x), (1, y)):
        rows = w_rows(place, c)
        send(w_ref.at[:, col((1 - c) * HALF + path * PATH, PATH)], wb.at[path, rows, :], sibling, W_SIB + path)
        keep(w_ref.at[:, col(c * HALF + path * PATH, PATH)], wb.at[path, rows, :], L_W + path)

    def forward_wx(k):
        for core in range(2):
            arrived(wx.at[w_rows(xx(3), core), pl.ds(k * CW, CW)], W_UP + 2 * k + core)
        for core in range(2):
            arrived(wx.at[w_rows(xx(1), core), pl.ds(k * CW, CW)], W_DOWN + 2 * k + core)
        below = wx.at[w_pair(xx(3)), pl.ds(k * CW, CW // 2)]
        above = wx.at[w_pair(xx(1)), pl.ds(k * CW + CW // 2, CW // 2)]
        send(below, below, at(z, xx(1), y, c), W_FUP + k)
        send(above, above, at(z, xx(3), y, c), W_FDOWN + k)

    def share_wy(place, group):
        first = wy.at[w_pair(place), col(mine, quad)]
        second = wy.at[w_pair(place), col(mine + quad, quad)]
        send(second, second, z_next, V_ZUP + group, when=has_next)
        send(first, first, z_prev, V_ZDOWN + group, when=has_one)
        send(second, second, z_prev, V_ZEDGE + group, V_ZUP + group, when=z == 1)
        send(first, first, z_next, V_ZEDGE + group, V_ZDOWN + group, when=z == Z - 2)

    def forward_wy_outer():
        for core in range(2):
            arrived(wy.at[w_rows(outer, core), col(mine, PATH // 2)], V_OUT + core)
        part_b = wy.at[w_pair(outer), col(mine + quad, quad)]
        send(part_b, part_b, y_pair, V_FIN)
        share_wy(outer, 0)

    def forward_wy_inner():
        for core in range(2):
            arrived(wy.at[w_rows(inner, core), col(mine, PATH // 2)], V_IN + core)
        part_a = wy.at[w_pair(inner), col(mine, quad)]
        send(part_a, part_a, at(z, x, outer, c), V_FOUT)
        share_wy(inner, 1)

    def forward_wy_far():
        arrived(wy.at[w_pair(yy(2)), col(mine + quad, quad)], V_FIN)
        arrived(wy.at[w_pair(yy(2)), col(mine, quad)], V_FOUT)
        share_wy(yy(2), 2)

    scaled = q_ref[...].astype(jnp.float32).T * SCALE
    coarse = scaled.astype(jnp.bfloat16)
    q2[:HD] = coarse
    q2[HD:] = (scaled - coarse.astype(jnp.float32)).astype(jnp.bfloat16)
    base = z * T
    local = lax.broadcasted_iota(jnp.int32, (8, T), 1)
    begin = jnp.zeros((8, T), jnp.int32)
    for d in range(DOCS):
        start = starts_ref[d]
        begin = jnp.where(local + base >= start, start, begin)
    lo_ref[...] = jnp.maximum(begin - base + WINDOW, local + 1)

    def scores(block, offset, k0, q0, width, span=TK, diagonal=False):
        keys = kn[block, pl.ds(k0, span), :]
        keys = jnp.concatenate([keys, keys], axis=1)
        values = jnp.concatenate(
            [kv[block, 1, :, pl.ds(k0, span)], jnp.ones((16, span), jnp.bfloat16)], axis=0
        )
        tiles = []
        spans = [(u + 1) * width if diagonal else span for u in range(2)]
        for u in range(2):
            columns = pl.ds(q0 + u * width, width)
            tiles.append(
                jnp.dot(keys[: spans[u]], q2[:, columns], preferred_element_type=jnp.float32)
            )
        for u in range(2):
            columns = pl.ds(q0 + u * width, width)
            place = lax.broadcasted_iota(jnp.int32, (spans[u], width), 0)
            allowed = place >= lo_ref[:1, columns] - (offset + k0)
            if diagonal:
                query = lax.broadcasted_iota(jnp.int32, (1, width), 1) + (q0 + u * width - k0)
                allowed &= place <= query
            tile = jnp.where(allowed, tiles[u], NEG)
            top = jnp.max(tile, axis=0, keepdims=True)
            if not diagonal:
                before = m_ref[:1, columns]
                top = jnp.maximum(before, top)
                keep_ = jnp.exp2(before - top)
            weights = jnp.exp2(tile - top).astype(jnp.bfloat16)
            added = jnp.dot(values[:, : spans[u]], weights, preferred_element_type=jnp.float32)
            m_ref[:1, columns] = top
            acc[:, columns] = added if diagonal else acc[:, columns] * keep_ + added

    half_t = T // 2
    arrived(piece(0, r ^ 2, half=0), KV_Y0)
    send(piece(0, r ^ 2, half=0), piece(0, r ^ 2, half=0), sibling, KV_CB0)
    arrived(piece(1, r, 0), KV_Z1, when=has_one)
    send(piece(1, r, 0), piece(1, r, 0), y_pair, KV_Y1, when=has_one)
    send(piece(1, r, 0), piece(2, r, 0), z_next, KV_Z2A, when=has_one & has_next)
    arrived(piece(0, r ^ 1, half=0), KV_CA0)
    arrived(piece(0, r ^ 3, half=0), KV_CB0)
    kn[0, pl.ds(0, half_t)] = kv[0, 0, :, pl.ds(0, half_t)].T
    scores(0, WINDOW, 0, 0, TQ, diagonal=True)
    arrived(piece(0, r ^ 2, half=1), KV_Y0 + 1)
    send(piece(0, r ^ 2, half=1), piece(0, r ^ 2, half=1), sibling, KV_CB0 + 1)
    arrived(piece(1, r, 1), KV_Z1 + 1, when=has_one)
    send(piece(1, r, 1), piece(1, r, 1), y_pair, KV_Y1 + 1, when=has_one)
    send(piece(1, r, 1), piece(2, r, 1), z_next, KV_Z2A + 1, when=has_one & has_next)
    send(piece(1, r), piece(1, r), sibling, KV_CA1, when=has_one)
    arrived(piece(0, r ^ 1, half=1), KV_CA0 + 1)
    arrived(piece(0, r ^ 3, half=1), KV_CB0 + 1)
    kn[0, pl.ds(half_t, half_t)] = kv[0, 0, :, pl.ds(half_t, half_t)].T
    scores(0, WINDOW, half_t, half_t, TQ, diagonal=True)
    arrived(piece(1, r ^ 2, 0), KV_Y1, when=has_one)
    send(piece(1, r ^ 2, 0), piece(2, r ^ 2, 0), z_next, KV_Z2B, when=has_one & has_next)
    scores(0, WINDOW, 0, half_t, TQ)

    arrived(piece(2, r, 1), KV_Z2A + 1, when=has_two)
    send(piece(2, r, 1), piece(2, r, 1), y_pair, KV_Y2, when=has_two)
    arrived(piece(1, r ^ 2, 1), KV_Y1 + 1, when=has_one)
    send(piece(1, r ^ 2), piece(1, r ^ 2), sibling, KV_CB1, when=has_one)
    arrived(piece(2, r, 0), KV_Z2A, when=has_two)
    send(piece(2, r), piece(2, r), sibling, KV_CA2, when=has_two)
    send_wy(inner, V_IN)
    forward_wx(0)
    arrived(piece(1, r ^ 1), KV_CA1, when=has_one)
    arrived(piece(1, r ^ 3), KV_CB1, when=has_one)

    for i in range(T // TK):

        @pl.when(has_one)
        def _():
            if i == 0:
                kn[1] = kv[1, 0].T

            @pl.loop(0, T // TK)
            def _(k):
                scores(1, T, pl.multiple_of(k * TK, TK), i * TK, TQ)

        if i == 0:
            for which, index in ((0, KV_Z2B), (1, KV_Y2)):
                arrived(piece(2, r ^ 2, which), index, when=has_two)
                send(piece(2, r ^ 2, which), piece(2, r ^ 2, which), sibling, KV_CB2 + which, when=has_two)
            forward_wx(1)
            forward_wy_outer()

    arrived(piece(2, r ^ 1), KV_CA2, when=has_two)
    arrived(piece(2, r ^ 3, 0), KV_CB2, when=has_two)
    arrived(piece(2, r ^ 3, 1), KV_CB2 + 1, when=has_two)

    @pl.when(has_two)
    def _():
        kn[2] = kv[2, 0].T

    att_x, att_y = att.at[0], att.at[1]
    x_slot, y_slot = w_rows(x, c), w_rows(y, c)

    def sub_rows(place):
        return pl.ds(pl.multiple_of(place * SUB, SUB), SUB)

    def forward_x(step):
        slot = att_x.at[:, w_rows(xx(4 - step), c)]
        arrived(slot, A_X + step - 1)
        send(slot, slot, sibling, A_XSIB + step)

    def forward_y(step, half):
        slot = w_rows(yy(4 - step), c)
        for i in (2 * half, 2 * half + 1):
            arrived(att_y.at[sub_rows(i), slot], A_Y + 4 * (step - 1) + i)
        both = att_y.at[pl.ds(2 * SUB * half, 2 * SUB), slot]
        send(both, both, sibling, A_YF + 2 * (step - 1) + half)

    for i, step in enumerate(ORDER):
        quarter = xx(step)
        q0 = pl.multiple_of(quarter * QT, QT)

        for place in range(X):

            @pl.when(has_two & (quarter == place))
            def _():
                scores(2, 0, place * QT, place * QT, QT // 2, span=T - place * QT)

        columns = pl.ds(q0, QT)
        total = acc[HD : HD + 1, columns]
        obuf[i] = (acc[:HD, columns] * (1.0 / total)).T.astype(jnp.bfloat16)
        if step:
            send(obuf.at[i], att_x.at[:, x_slot], at(z, quarter, y, c), A_X + step - 1)
        else:
            send(obuf.at[i], att_x.at[:, x_slot], sibling, A_XSIB)
            keep(obuf.at[i], att_x.at[:, x_slot], L_ATT)
        for away in (2, 1, 3):
            send(
                obuf.at[i, sub_rows(yy(away)), :],
                att_y.at[sub_rows(i), y_slot],
                at(z, x, yy(away), c),
                A_Y + 4 * (away - 1) + i,
            )
        send(obuf.at[i, sub_rows(y), :], att_y.at[sub_rows(i), y_slot], sibling, A_YOWN + i)
        keep(obuf.at[i, sub_rows(y), :], att_y.at[sub_rows(i), y_slot], L_ATT + 1 + i)
        if i == 1:
            forward_wy_inner()
        if i == 2:
            forward_x(2)
            for away in (2, 1, 3):
                forward_y(away, 0)
    for away in (1, 3):
        forward_x(away)
    for away in (2, 1, 3):
        forward_y(away, 1)
    forward_wy_far()
    arrived(wx.at[w_rows(x, 1 - c), :], W_SIB)
    arrived(wy.at[w_rows(y, 1 - c), :], W_SIB + 1)
    for one in kept:
        one.wait()
    del kept[:]
    for step in range(4):
        arrived(att_x.at[:, w_rows(xx(4 - step), 1 - c)], A_XSIB + step)

    left, right = pl.ds(0, CW // 2), pl.ds(CW // 2, CW // 2)
    def device(path, step):
        return at(z, x, yy(step), c) if path == 0 else at(z, xx(step), y, c)

    def chunk_of(path, k):
        return k * CW if path == 0 else (mine if k == 0 else theirs)

    def sub(j, block, half):
        return part[j, sub_rows(block), half]

    def block_of(path, step):
        return yy(step) if path == 0 else ORDER.index(step)

    def project(path, k):
        j = 2 * k + path
        if path == 0:
            arrived(wx.at[w_pair(xx(2)), pl.ds(k * CW, CW // 2)], W_FUP + k)
            arrived(wx.at[w_pair(xx(2)), pl.ds(k * CW + CW // 2, CW // 2)], W_FDOWN + k)
        elif k == 1:
            for group, place in enumerate((outer, inner, yy(2))):
                arrived(wy.at[w_pair(place), col(theirs + quad, quad)], V_ZUP + group)
                arrived(wy.at[w_pair(place), col(theirs, quad)], V_ZDOWN + group)
        step = R_UP + 7 * j
        if path == 1 and k == 0:
            for i in range(4):
                arrived(att_y.at[sub_rows(i), w_rows(y, 1 - c)], A_YOWN + i)
            for away in (1, 2, 3):
                for half in range(2):
                    both = att_y.at[pl.ds(2 * SUB * half, 2 * SUB), w_rows(yy(4 - away), 1 - c)]
                    arrived(both, A_YF + 2 * (away - 1) + half)
        weight = wb[path, :, col(chunk_of(path, k), CW)]
        part[j] = jnp.dot(att[path], weight, preferred_element_type=jnp.float32)
        rel[j, 0] = sub(j, block_of(path, 2), left).astype(jnp.bfloat16)
        send(rel.at[j, 0], rin.at[j, 0], device(path, 1), step)
        rel[j, 1] = sub(j, block_of(path, 2), right).astype(jnp.bfloat16)
        send(rel.at[j, 1], rin.at[j, 1], device(path, 3), step + 1)
        msg[j, 0] = sub(j, block_of(path, 1), right).astype(jnp.bfloat16)
        send(msg.at[j, 0], min_.at[j, 0], device(path, 1), step + 2)
        msg[j, 1] = sub(j, block_of(path, 3), left).astype(jnp.bfloat16)
        send(msg.at[j, 1], min_.at[j, 1], device(path, 3), step + 3)

    def relay(path, k):
        j = 2 * k + path
        step = R_UP + 7 * j
        arrived(rin.at[j, 0], step)
        msg[j, 2] = (sub(j, block_of(path, 1), left) + rin[j, 0].astype(jnp.float32)).astype(jnp.bfloat16)
        send(msg.at[j, 2], min_.at[j, 2], device(path, 1), step + 4)
        arrived(rin.at[j, 1], step + 1)
        msg[j, 3] = (sub(j, block_of(path, 3), right) + rin[j, 1].astype(jnp.float32)).astype(jnp.bfloat16)
        send(msg.at[j, 3], min_.at[j, 3], device(path, 3), step + 5)

    def finish(path, k):
        j = 2 * k + path
        step = R_UP + 7 * j
        for one in range(4):
            arrived(min_.at[j, one], step + 2 + one)
        for columns, first, second in ((left, 1, 2), (right, 0, 3)):
            total = sub(j, block_of(path, 0), columns) + min_[j, first].astype(jnp.float32)
            total += min_[j, second].astype(jnp.float32)
            res[j, :, columns] = total.astype(jnp.bfloat16)
        place = out_ref.at[:, col(c * HALF + path * PATH + chunk_of(path, k), CW)]
        rows = SUB // 2
        keep(res.at[j, pl.ds(pl.multiple_of(c * rows, rows), rows), :], place, L_OUT + j)
        other = pl.ds(pl.multiple_of((1 - c) * rows, rows), rows)
        send(res.at[j, other, :], place, sibling, step + 6)

    order = [(path, k) for k in range(NC) for path in range(2)]
    for n in range(len(order) + 4):
        if n < len(order):
            project(*order[n])
        if 2 <= n < len(order) + 2:
            relay(*order[n - 2])
        if n >= 4:
            finish(*order[n - 4])
    for path, k in order:
        place = out_ref.at[:, col((1 - c) * HALF + path * PATH + chunk_of(path, k), CW)]
        arrived(place, R_UP + 7 * (2 * k + path) + 6)
    for one in kept:
        one.wait()
    for one, when in sent:
        do(one.wait_send, when)


def on_device(queries, keys, values, out_weight, doc_starts):
    bf16, f32 = jnp.bfloat16, jnp.float32
    vmem = pl.BlockSpec(memory_space=pltpu.VMEM)
    return pl.pallas_call(
        kernel,
        out_shape=jax.ShapeDtypeStruct((SUB // 2, D), bf16),
        in_specs=[pl.BlockSpec(memory_space=pltpu.SMEM), vmem, vmem, vmem, pl.BlockSpec(memory_space=pl.ANY)],
        out_specs=pl.BlockSpec(memory_space=pl.ANY),
        scratch_shapes=[
            pltpu.VMEM((3, 2, HD, T), bf16),
            pltpu.VMEM((3, T, HD), bf16),
            pltpu.VMEM((2 * HD, T), bf16),
            pltpu.VMEM((8, T), jnp.int32),
            pltpu.VMEM((8, T), f32),
            pltpu.VMEM((HD + 16, T), f32),
            pltpu.VMEM((X, QT, HD), bf16),
            pltpu.VMEM((2, QT, 2 * X * HD), bf16),
            pltpu.VMEM((2, 2 * X * HD, PATH), bf16),
            pltpu.VMEM((2 * NC, QT, CW), f32),
            pltpu.VMEM((2 * NC, 2, SUB, CW // 2), bf16),
            pltpu.VMEM((2 * NC, 2, SUB, CW // 2), bf16),
            pltpu.VMEM((2 * NC, 4, SUB, CW // 2), bf16),
            pltpu.VMEM((2 * NC, 4, SUB, CW // 2), bf16),
            pltpu.VMEM((2 * NC, SUB, CW), bf16),
            pltpu.SemaphoreType.DMA((N_COPIES,)),
            pltpu.SemaphoreType.DMA((N_COPIES,)),
            pltpu.SemaphoreType.DMA((N_LOCAL,)),
        ],
        compiler_params=pltpu.CompilerParams(
            collective_id=0, has_side_effects=True, vmem_limit_bytes=56 * 2**20
        ),
    )(doc_starts, queries, keys.T, values.T, out_weight)


def solution(mesh):
    placed = (P("ctx", "head"), P("ctx", "head"), P("ctx", "head"), P("head", None), P())
    return jax.shard_map(
        on_device, mesh=mesh, in_specs=placed, out_specs=P(("ctx", "head"), None), check_vma=False
    )
```

```python
import jax
import jax.numpy as jnp
from jax import lax
from jax.experimental import pallas as pl
from jax.experimental.pallas import tpu as pltpu
from jax.sharding import PartitionSpec as P

GROUP = 4
WINDOW = 4096
T = 2048
HD = 128
D = 4096
DOCS = 16
Z, X, Y = 8, 4, 4
HALF = D // 2
PATH = HALF // 2
CW = 512
NC = PATH // CW
QT = T // X
SUB = QT // Y
TQ = 512
TK = 1024
NEG = -1e30
SCALE = 1.4426950408889634 * HD**-0.5

ORDER = (2, 1, 3, 0)

KV_Y0, KV_Y1, KV_Y2, KV_Z1, KV_Z2A, KV_Z2B = 0, 2, 4, 5, 7, 9
KV_CA0, KV_CB0, KV_CA1, KV_CB1, KV_CA2, KV_CB2 = 10, 12, 14, 15, 16, 17
W_UP, W_DOWN, W_FUP, W_FDOWN, W_SIB = 19, 23, 27, 29, 31
V_IN, V_OUT, V_FIN, V_FOUT, V_ZUP, V_ZDOWN, V_ZEDGE = 33, 35, 37, 38, 39, 42, 45
A_X, A_Y, A_XSIB, A_YOWN, A_YF = 48, 51, 63, 67, 71
R_UP = 77
N_COPIES = R_UP + 7 * 2 * NC
L_W, L_ATT, L_OUT = 0, 2, 7
N_LOCAL = L_OUT + 2 * NC


def kernel(
    starts_ref, q_ref, k_ref, v_ref, w_ref, out_ref,
    kv, kn, q2, lo_ref, m_ref, acc, obuf, att, wb, part, rel, rin, msg, min_, res,
    ssem, rsem, lsem,
):
    z = lax.axis_index("ctx")
    head = lax.axis_index("head")
    c = lax.rem(head, 2)
    y = lax.rem(head // 2, Y)
    x = head // (2 * Y)
    r = lax.rem(head, GROUP)
    odd_y, odd_z = lax.rem(y, 2), lax.rem(z, 2)

    def at(z_, x_, y_, c_):
        return (z_, (x_ * Y + y_) * 2 + c_)

    def xx(step):
        return lax.rem(x + step, X)

    def yy(step):
        return lax.rem(y + step, Y)

    z_next = at(lax.rem(z + 1, Z), x, y, c)
    z_prev = at(lax.rem(z + Z - 1, Z), x, y, c)
    has_next, has_one, has_two = z < Z - 1, z >= 1, z >= 2
    sibling = at(z, x, y, 1 - c)
    inner = yy(1 + 2 * odd_y)
    outer = yy(3 - 2 * odd_y)
    y_pair = at(z, x, inner, c)

    def copy(src, dst, device, send, recv):
        return pltpu.make_async_remote_copy(
            src_ref=src,
            dst_ref=dst,
            send_sem=ssem.at[send],
            recv_sem=rsem.at[recv],
            device_id=device,
            device_id_type=pl.DeviceIdType.MESH,
        )

    def do(action, when):
        if when is None:
            action()
        else:
            pl.when(when)(action)

    sent = []
    kept = []

    def send(src, dst, device, index, recv=None, when=None):
        one = copy(src, dst, device, index, index if recv is None else recv)
        do(one.start, when)
        sent.append((one, when))

    def keep(src, dst, index):
        one = pltpu.make_async_copy(src, dst, lsem.at[index])
        one.start()
        kept.append(one)

    def arrived(dst, index, when=None):
        do(copy(dst, dst, sibling, 0, index).wait_recv, when)

    def piece(block, member, which=None, half=None):
        rows = pl.ds(pl.multiple_of(32 * member, 32), 32)
        tokens = pl.ds(0, T) if half is None else pl.ds(half * (T // 2), T // 2)
        return kv.at[block, :, rows, tokens] if which is None else kv.at[block, which, rows, tokens]

    def w_rows(place, core):
        return pl.ds(pl.multiple_of(HD * (2 * place + core), HD), HD)

    def w_pair(place):
        return pl.ds(pl.multiple_of(2 * HD * place, 2 * HD), 2 * HD)

    def col(start, width):
        return pl.ds(pl.multiple_of(start, 128), width)

    partners = [(sibling, None), (z_next, has_next), (z_prev, has_one)]
    partners += [(at(z, x, yy(step), core), None) for step in (1, 3) for core in range(2)]
    partners += [(at(z, xx(step), y, core), None) for step in (1, 3) for core in range(2)]
    partners += [(at(z, x, yy(2), c), None), (at(z, xx(2), y, c), None)]
    barrier = pltpu.get_barrier_semaphore()
    for device, when in partners:

        def greet(device=device):
            pl.semaphore_signal(barrier, inc=1, device_id=device, device_id_type=pl.DeviceIdType.MESH)

        do(greet, when)
    own = pl.ds(pl.multiple_of(32 * r, 32), 32)
    kv[0, 0, own, :] = k_ref[...]
    kv[0, 1, own, :] = v_ref[...]
    at_edge = jnp.where(has_next, 0, 1) + jnp.where(has_one, 0, 1)
    pl.semaphore_wait(barrier, len(partners) - at_edge)

    send(piece(0, r, half=0), piece(0, r, half=0), y_pair, KV_Y0)
    send(piece(0, r, 0), piece(1, r, 0), z_next, KV_Z1, when=has_next)
    send(piece(0, r, half=0), piece(0, r, half=0), sibling, KV_CA0)
    send(piece(0, r, half=1), piece(0, r, half=1), y_pair, KV_Y0 + 1)
    send(piece(0, r, 1), piece(1, r, 1), z_next, KV_Z1 + 1, when=has_next)
    send(piece(0, r, half=1), piece(0, r, half=1), sibling, KV_CA0 + 1)
    wx, wy = wb.at[0], wb.at[1]
    for k in range(NC):
        for half in range(2):
            src = w_ref.at[:, pl.ds(half * HALF + k * CW, CW)]
            dst = wx.at[w_rows(x, c), pl.ds(k * CW, CW)]
            send(src, dst, at(z, xx(1), y, half), W_UP + 2 * k + half, W_UP + 2 * k + c)
            send(src, dst, at(z, xx(3), y, half), W_DOWN + 2 * k + half, W_DOWN + 2 * k + c)
    mine, theirs = odd_z * (PATH // 2), (1 - odd_z) * (PATH // 2)
    quad = PATH // 4

    def send_wy(place, first):
        for half in range(2):
            src = w_ref.at[:, col(half * HALF + PATH + mine, PATH // 2)]
            dst = wy.at[w_rows(y, c), col(mine, PATH // 2)]
            send(src, dst, at(z, x, place, half), first + half, first + c)

    send_wy(outer, V_OUT)
    for path, place in ((0, x), (1, y)):
        rows = w_rows(place, c)
        send(w_ref.at[:, col((1 - c) * HALF + path * PATH, PATH)], wb.at[path, rows, :], sibling, W_SIB + path)
        keep(w_ref.at[:, col(c * HALF + path * PATH, PATH)], wb.at[path, rows, :], L_W + path)

    def forward_wx(k):
        for core in range(2):
            arrived(wx.at[w_rows(xx(3), core), pl.ds(k * CW, CW)], W_UP + 2 * k + core)
        for core in range(2):
            arrived(wx.at[w_rows(xx(1), core), pl.ds(k * CW, CW)], W_DOWN + 2 * k + core)
        below = wx.at[w_pair(xx(3)), pl.ds(k * CW, CW // 2)]
        above = wx.at[w_pair(xx(1)), pl.ds(k * CW + CW // 2, CW // 2)]
        send(below, below, at(z, xx(1), y, c), W_FUP + k)
        send(above, above, at(z, xx(3), y, c), W_FDOWN + k)

    def share_wy(place, group):
        first = wy.at[w_pair(place), col(mine, quad)]
        second = wy.at[w_pair(place), col(mine + quad, quad)]
        send(second, second, z_next, V_ZUP + group, when=has_next)
        send(first, first, z_prev, V_ZDOWN + group, when=has_one)
        send(second, second, z_prev, V_ZEDGE + group, V_ZUP + group, when=z == 1)
        send(first, first, z_next, V_ZEDGE + group, V_ZDOWN + group, when=z == Z - 2)

    def forward_wy_outer():
        for core in range(2):
            arrived(wy.at[w_rows(outer, core), col(mine, PATH // 2)], V_OUT + core)
        part_b = wy.at[w_pair(outer), col(mine + quad, quad)]
        send(part_b, part_b, y_pair, V_FIN)
        share_wy(outer, 0)

    def forward_wy_inner():
        for core in range(2):
            arrived(wy.at[w_rows(inner, core), col(mine, PATH // 2)], V_IN + core)
        part_a = wy.at[w_pair(inner), col(mine, quad)]
        send(part_a, part_a, at(z, x, outer, c), V_FOUT)
        share_wy(inner, 1)

    def forward_wy_far():
        arrived(wy.at[w_pair(yy(2)), col(mine + quad, quad)], V_FIN)
        arrived(wy.at[w_pair(yy(2)), col(mine, quad)], V_FOUT)
        share_wy(yy(2), 2)

    scaled = q_ref[...].astype(jnp.float32).T * SCALE
    coarse = scaled.astype(jnp.bfloat16)
    q2[:HD] = coarse
    q2[HD:] = (scaled - coarse.astype(jnp.float32)).astype(jnp.bfloat16)
    base = z * T
    local = lax.broadcasted_iota(jnp.int32, (8, T), 1)
    begin = jnp.zeros((8, T), jnp.int32)
    for d in range(DOCS):
        start = starts_ref[d]
        begin = jnp.where(local + base >= start, start, begin)
    lo_ref[...] = jnp.maximum(begin - base + WINDOW, local + 1)

    def scores(block, offset, k0, q0, width, span=TK, diagonal=False):
        keys = kn[block, pl.ds(k0, span), :]
        keys = jnp.concatenate([keys, keys], axis=1)
        values = jnp.concatenate(
            [kv[block, 1, :, pl.ds(k0, span)], jnp.ones((16, span), jnp.bfloat16)], axis=0
        )
        tiles = []
        spans = [(u + 1) * width if diagonal else span for u in range(2)]
        for u in range(2):
            columns = pl.ds(q0 + u * width, width)
            tiles.append(
                jnp.dot(keys[: spans[u]], q2[:, columns], preferred_element_type=jnp.float32)
            )
        for u in range(2):
            columns = pl.ds(q0 + u * width, width)
            place = lax.broadcasted_iota(jnp.int32, (spans[u], width), 0)
            allowed = place >= lo_ref[:1, columns] - (offset + k0)
            if diagonal:
                query = lax.broadcasted_iota(jnp.int32, (1, width), 1) + (q0 + u * width - k0)
                allowed &= place <= query
            tile = jnp.where(allowed, tiles[u], NEG)
            top = jnp.max(tile, axis=0, keepdims=True)
            if not diagonal:
                before = m_ref[:1, columns]
                top = jnp.maximum(before, top)
                keep_ = jnp.exp2(before - top)
            weights = jnp.exp2(tile - top).astype(jnp.bfloat16)
            added = jnp.dot(values[:, : spans[u]], weights, preferred_element_type=jnp.float32)
            m_ref[:1, columns] = top
            acc[:, columns] = added if diagonal else acc[:, columns] * keep_ + added

    half_t = T // 2
    arrived(piece(0, r ^ 2, half=0), KV_Y0)
    send(piece(0, r ^ 2, half=0), piece(0, r ^ 2, half=0), sibling, KV_CB0)
    arrived(piece(1, r, 0), KV_Z1, when=has_one)
    send(piece(1, r, 0), piece(1, r, 0), y_pair, KV_Y1, when=has_one)
    send(piece(1, r, 0), piece(2, r, 0), z_next, KV_Z2A, when=has_one & has_next)
    arrived(piece(0, r ^ 1, half=0), KV_CA0)
    arrived(piece(0, r ^ 3, half=0), KV_CB0)
    kn[0, pl.ds(0, half_t)] = kv[0, 0, :, pl.ds(0, half_t)].T
    scores(0, WINDOW, 0, 0, TQ, diagonal=True)
    arrived(piece(0, r ^ 2, half=1), KV_Y0 + 1)
    send(piece(0, r ^ 2, half=1), piece(0, r ^ 2, half=1), sibling, KV_CB0 + 1)
    arrived(piece(1, r, 1), KV_Z1 + 1, when=has_one)
    send(piece(1, r, 1), piece(1, r, 1), y_pair, KV_Y1 + 1, when=has_one)
    send(piece(1, r, 1), piece(2, r, 1), z_next, KV_Z2A + 1, when=has_one & has_next)
    send(piece(1, r), piece(1, r), sibling, KV_CA1, when=has_one)
    arrived(piece(0, r ^ 1, half=1), KV_CA0 + 1)
    arrived(piece(0, r ^ 3, half=1), KV_CB0 + 1)
    kn[0, pl.ds(half_t, half_t)] = kv[0, 0, :, pl.ds(half_t, half_t)].T
    scores(0, WINDOW, half_t, half_t, TQ, diagonal=True)
    arrived(piece(1, r ^ 2, 0), KV_Y1, when=has_one)
    send(piece(1, r ^ 2, 0), piece(2, r ^ 2, 0), z_next, KV_Z2B, when=has_one & has_next)
    scores(0, WINDOW, 0, half_t, TQ)

    arrived(piece(2, r, 1), KV_Z2A + 1, when=has_two)
    send(piece(2, r, 1), piece(2, r, 1), y_pair, KV_Y2, when=has_two)
    arrived(piece(1, r ^ 2, 1), KV_Y1 + 1, when=has_one)
    send(piece(1, r ^ 2), piece(1, r ^ 2), sibling, KV_CB1, when=has_one)
    arrived(piece(2, r, 0), KV_Z2A, when=has_two)
    send(piece(2, r), piece(2, r), sibling, KV_CA2, when=has_two)
    send_wy(inner, V_IN)
    forward_wx(0)
    arrived(piece(1, r ^ 1), KV_CA1, when=has_one)
    arrived(piece(1, r ^ 3), KV_CB1, when=has_one)

    for i in range(T // TK):

        @pl.when(has_one)
        def _():
            if i == 0:
                kn[1] = kv[1, 0].T

            @pl.loop(0, T // TK)
            def _(k):
                scores(1, T, pl.multiple_of(k * TK, TK), i * TK, TQ)

        if i == 0:
            for which, index in ((0, KV_Z2B), (1, KV_Y2)):
                arrived(piece(2, r ^ 2, which), index, when=has_two)
                send(piece(2, r ^ 2, which), piece(2, r ^ 2, which), sibling, KV_CB2 + which, when=has_two)
            forward_wx(1)
            forward_wy_outer()

    arrived(piece(2, r ^ 1), KV_CA2, when=has_two)
    arrived(piece(2, r ^ 3, 0), KV_CB2, when=has_two)
    arrived(piece(2, r ^ 3, 1), KV_CB2 + 1, when=has_two)

    @pl.when(has_two)
    def _():
        kn[2] = kv[2, 0].T

    att_x, att_y = att.at[0], att.at[1]
    x_slot, y_slot = w_rows(x, c), w_rows(y, c)

    def sub_rows(place):
        return pl.ds(pl.multiple_of(place * SUB, SUB), SUB)

    def forward_x(step):
        slot = att_x.at[:, w_rows(xx(4 - step), c)]
        arrived(slot, A_X + step - 1)
        send(slot, slot, sibling, A_XSIB + step)

    def forward_y(step, half):
        slot = w_rows(yy(4 - step), c)
        for i in (2 * half, 2 * half + 1):
            arrived(att_y.at[sub_rows(i), slot], A_Y + 4 * (step - 1) + i)
        both = att_y.at[pl.ds(2 * SUB * half, 2 * SUB), slot]
        send(both, both, sibling, A_YF + 2 * (step - 1) + half)

    for i, step in enumerate(ORDER):
        quarter = xx(step)
        q0 = pl.multiple_of(quarter * QT, QT)

        for place in range(X):

            @pl.when(has_two & (quarter == place))
            def _():
                scores(2, 0, place * QT, place * QT, QT // 2, span=T - place * QT)

        columns = pl.ds(q0, QT)
        total = acc[HD : HD + 1, columns]
        obuf[i] = (acc[:HD, columns] * (1.0 / total)).T.astype(jnp.bfloat16)
        if step:
            send(obuf.at[i], att_x.at[:, x_slot], at(z, quarter, y, c), A_X + step - 1)
        else:
            send(obuf.at[i], att_x.at[:, x_slot], sibling, A_XSIB)
            keep(obuf.at[i], att_x.at[:, x_slot], L_ATT)
        for away in (2, 1, 3):
            send(
                obuf.at[i, sub_rows(yy(away)), :],
                att_y.at[sub_rows(i), y_slot],
                at(z, x, yy(away), c),
                A_Y + 4 * (away - 1) + i,
            )
        send(obuf.at[i, sub_rows(y), :], att_y.at[sub_rows(i), y_slot], sibling, A_YOWN + i)
        keep(obuf.at[i, sub_rows(y), :], att_y.at[sub_rows(i), y_slot], L_ATT + 1 + i)
        if i == 1:
            forward_wy_inner()
        if i == 2:
            forward_x(2)
            for away in (2, 1, 3):
                forward_y(away, 0)
    forward_wy_far()
    for away in (1, 3):
        forward_x(away)
    for away in (2, 1, 3):
        forward_y(away, 1)
    arrived(wx.at[w_rows(x, 1 - c), :], W_SIB)
    arrived(wy.at[w_rows(y, 1 - c), :], W_SIB + 1)
    for one in kept:
        one.wait()
    del kept[:]
    for step in range(4):
        arrived(att_x.at[:, w_rows(xx(4 - step), 1 - c)], A_XSIB + step)

    left, right = pl.ds(0, CW // 2), pl.ds(CW // 2, CW // 2)
    def device(path, step):
        return at(z, x, yy(step), c) if path == 0 else at(z, xx(step), y, c)

    def chunk_of(path, k):
        return k * CW if path == 0 else (mine if k == 0 else theirs)

    def sub(j, block, half):
        return part[j, sub_rows(block), half]

    def block_of(path, step):
        return yy(step) if path == 0 else ORDER.index(step)

    def project(path, k):
        j = 2 * k + path
        if path == 0:
            arrived(wx.at[w_pair(xx(2)), pl.ds(k * CW, CW // 2)], W_FUP + k)
            arrived(wx.at[w_pair(xx(2)), pl.ds(k * CW + CW // 2, CW // 2)], W_FDOWN + k)
        elif k == 1:
            for group, place in enumerate((outer, inner, yy(2))):
                arrived(wy.at[w_pair(place), col(theirs + quad, quad)], V_ZUP + group)
                arrived(wy.at[w_pair(place), col(theirs, quad)], V_ZDOWN + group)
        step = R_UP + 7 * j
        if path == 1 and k == 0:
            for i in range(4):
                arrived(att_y.at[sub_rows(i), w_rows(y, 1 - c)], A_YOWN + i)
            for away in (1, 2, 3):
                for half in range(2):
                    both = att_y.at[pl.ds(2 * SUB * half, 2 * SUB), w_rows(yy(4 - away), 1 - c)]
                    arrived(both, A_YF + 2 * (away - 1) + half)
        weight = wb[path, :, col(chunk_of(path, k), CW)]
        part[j] = jnp.dot(att[path], weight, preferred_element_type=jnp.float32)
        rel[j, 0] = sub(j, block_of(path, 2), left).astype(jnp.bfloat16)
        send(rel.at[j, 0], rin.at[j, 0], device(path, 1), step)
        rel[j, 1] = sub(j, block_of(path, 2), right).astype(jnp.bfloat16)
        send(rel.at[j, 1], rin.at[j, 1], device(path, 3), step + 1)
        msg[j, 0] = sub(j, block_of(path, 1), right).astype(jnp.bfloat16)
        send(msg.at[j, 0], min_.at[j, 0], device(path, 1), step + 2)
        msg[j, 1] = sub(j, block_of(path, 3), left).astype(jnp.bfloat16)
        send(msg.at[j, 1], min_.at[j, 1], device(path, 3), step + 3)

    def relay(path, k):
        j = 2 * k + path
        step = R_UP + 7 * j
        arrived(rin.at[j, 0], step)
        msg[j, 2] = (sub(j, block_of(path, 1), left) + rin[j, 0].astype(jnp.float32)).astype(jnp.bfloat16)
        send(msg.at[j, 2], min_.at[j, 2], device(path, 1), step + 4)
        arrived(rin.at[j, 1], step + 1)
        msg[j, 3] = (sub(j, block_of(path, 3), right) + rin[j, 1].astype(jnp.float32)).astype(jnp.bfloat16)
        send(msg.at[j, 3], min_.at[j, 3], device(path, 3), step + 5)

    def finish(path, k):
        j = 2 * k + path
        step = R_UP + 7 * j
        for one in range(4):
            arrived(min_.at[j, one], step + 2 + one)
        for columns, first, second in ((left, 1, 2), (right, 0, 3)):
            total = sub(j, block_of(path, 0), columns) + min_[j, first].astype(jnp.float32)
            total += min_[j, second].astype(jnp.float32)
            res[j, :, columns] = total.astype(jnp.bfloat16)
        place = out_ref.at[:, col(c * HALF + path * PATH + chunk_of(path, k), CW)]
        rows = SUB // 2
        keep(res.at[j, pl.ds(pl.multiple_of(c * rows, rows), rows), :], place, L_OUT + j)
        other = pl.ds(pl.multiple_of((1 - c) * rows, rows), rows)
        send(res.at[j, other, :], place, sibling, step + 6)

    order = [(path, k) for k in range(NC) for path in range(2)]
    for n in range(len(order) + 4):
        if n < len(order):
            project(*order[n])
        if 2 <= n < len(order) + 2:
            relay(*order[n - 2])
        if n >= 4:
            finish(*order[n - 4])
    for path, k in order:
        place = out_ref.at[:, col((1 - c) * HALF + path * PATH + chunk_of(path, k), CW)]
        arrived(place, R_UP + 7 * (2 * k + path) + 6)
    for one in kept:
        one.wait()
    for one, when in sent:
        do(one.wait_send, when)


def on_device(queries, keys, values, out_weight, doc_starts):
    bf16, f32 = jnp.bfloat16, jnp.float32
    vmem = pl.BlockSpec(memory_space=pltpu.VMEM)
    return pl.pallas_call(
        kernel,
        out_shape=jax.ShapeDtypeStruct((SUB // 2, D), bf16),
        in_specs=[pl.BlockSpec(memory_space=pltpu.SMEM), vmem, vmem, vmem, pl.BlockSpec(memory_space=pl.ANY)],
        out_specs=pl.BlockSpec(memory_space=pl.ANY),
        scratch_shapes=[
            pltpu.VMEM((3, 2, HD, T), bf16),
            pltpu.VMEM((3, T, HD), bf16),
            pltpu.VMEM((2 * HD, T), bf16),
            pltpu.VMEM((8, T), jnp.int32),
            pltpu.VMEM((8, T), f32),
            pltpu.VMEM((HD + 16, T), f32),
            pltpu.VMEM((X, QT, HD), bf16),
            pltpu.VMEM((2, QT, 2 * X * HD), bf16),
            pltpu.VMEM((2, 2 * X * HD, PATH), bf16),
            pltpu.VMEM((2 * NC, QT, CW), f32),
            pltpu.VMEM((2 * NC, 2, SUB, CW // 2), bf16),
            pltpu.VMEM((2 * NC, 2, SUB, CW // 2), bf16),
            pltpu.VMEM((2 * NC, 4, SUB, CW // 2), bf16),
            pltpu.VMEM((2 * NC, 4, SUB, CW // 2), bf16),
            pltpu.VMEM((2 * NC, SUB, CW), bf16),
            pltpu.SemaphoreType.DMA((N_COPIES,)),
            pltpu.SemaphoreType.DMA((N_COPIES,)),
            pltpu.SemaphoreType.DMA((N_LOCAL,)),
        ],
        compiler_params=pltpu.CompilerParams(
            collective_id=0, has_side_effects=True, vmem_limit_bytes=56 * 2**20
        ),
    )(doc_starts, queries, keys.T, values.T, out_weight)


def solution(mesh):
    placed = (P("ctx", "head"), P("ctx", "head"), P("ctx", "head"), P("head", None), P())
    return jax.shard_map(
        on_device, mesh=mesh, in_specs=placed, out_specs=P(("ctx", "head"), None), check_vma=False
    )
```
